32 devices in a mesh: band: 2 (over y), gx: 4 (over z), gy: 2 (over x), gz: 2 (over core).
Axes of the slice: x: 2, y: 2, z: 4, core: 2. Of those that a mesh axis runs over, the one named last changes fastest.
Arguments:
- csm: bfloat16 [2, 4, 512, 512], P(None, 'band', ('gx', 'gy', 'gz')), parts along dimension 1, may hold values from -6 to 6
- positions: float32 [3, 512], replicated, may hold values from -1 to 1
- mic_order: int32 [512], replicated, may hold values from 0 to 511, each once
- wavenumbers: float32 [4], P('band'), parts along dimension 0, may hold values from 20 to 60
Outputs:
- beam_map: float32 [32, 16, 128], P(('band', 'gx'), ('gy', 'gz')), parts along dimension 0
- source_map: float32 [32, 16, 128], P(('band', 'gx'), ('gy', 'gz')), parts along dimension 0
The draws below stay inside these ranges and needn't reach their ends.
There are 2 independent parts, one for each index of `band`. The reference program is written for one: setup_inputs(seed, part) draws one part's arguments, and reference() takes and returns one part's arrays. A program takes and returns all parts, laid end to end along the dimension named above; an argument that names none is the same for every part. Nothing has to cross between parts.
Inputs may be any that keep to these rules, and one draw needn't show every extreme that they name: mic_order names each microphone once.
All inputs are finite; a program needn't handle non-finite values.
Results may differ from the reference program's by a relative error of at most 0.0055.
Values may be sent and summed in bfloat16 or wider, within the bound.
A program may use at most 64 MiB of HBM per device.

```python
import math
import jax
import jax.numpy as jnp
from jax import lax

M = 512
NY = 128
BINS = 2
ITERS = 3
NX = 16
NZ = 16


def level_of(own_key, shape, pieces, least, largest):
    def one(axis_at, shards_of):
        heights = jax.random.uniform(jax.random.fold_in(jax.random.fold_in(own_key, 6), axis_at), (shards_of,), jnp.float32, least / len(pieces), largest / len(pieces))
        return jnp.repeat(jnp.exp(heights), shape[axis_at] // shards_of).reshape((-1,) + (1,) * (len(shape) - axis_at - 1))

    level = one(*pieces[0])
    for cut in pieces[1:]:
        level = level * one(*cut)
    return level


def noise(rng, extent, scale, most, cuts=(), kind=jnp.bfloat16):
    values = scale * jax.random.normal(rng, extent, jnp.float32)
    if cuts:
        values = values * level_of(rng, extent, cuts, -0.22, 0.18)
    return jnp.clip(values, -most, most).astype(kind)


def setup_inputs(seed: int = 0, part: int = 0) -> dict:
    splits = jax.random.split(jax.random.key(seed), 5)
    own_keys = jax.random.split(jax.random.fold_in(splits[4], part), 5)
    return {
        "csm": noise(own_keys[0], (2, BINS, M, M), 1.0, 6.0, ((2, 16),)),
        "positions": jnp.clip(jax.random.uniform(splits[1], (3, M), jnp.float32, -1.0, 1.0), -1.0, 1.0),
        "mic_order": jax.random.permutation(splits[2], M).astype(jnp.int32),
        "wavenumbers": jnp.clip(jnp.exp(jax.random.uniform(own_keys[3], (BINS,), jnp.float32, math.log(20.0), math.log(60.0))), 20.0, 60.0),
    }


def coords_plane(index, length):
    return (2.0 * index.astype(jnp.float32) + 1.0) / length - 1.0

def coords_depth(index, length):
    return 2.0 + (index.astype(jnp.float32) + 0.5) / length

def steering(cells, placed, rate, factor):
    diff_x = cells[0][None, :] - placed[0][:, None]
    diff_y = cells[1][None, :] - placed[1][:, None]
    diff_z = cells[2][None, :] - placed[2][:, None]
    dist = jnp.sqrt(diff_x * diff_x + diff_y * diff_y + diff_z * diff_z)
    phase = rate * dist
    return ((jnp.cos(phase) * factor).astype(jnp.bfloat16), (-jnp.sin(phase) * factor).astype(jnp.bfloat16))

def reference(csm, positions, mic_order, wavenumbers):
    highest = lax.Precision.HIGHEST
    factor = 1.0 / math.sqrt(M)
    placed = jnp.take(positions, mic_order, axis=1)
    y_coords = coords_plane(jnp.arange(NY, dtype=jnp.int32), NY)
    z_coords = coords_depth(jnp.arange(NZ, dtype=jnp.int32), NZ)
    centre = jnp.stack([coords_plane(jnp.full((1,), NX // 2, jnp.int32), NX), coords_plane(jnp.full((1,), NY // 2, jnp.int32), NY), coords_depth(jnp.full((1,), NZ // 2, jnp.int32), NZ)])
    centre_rows = []
    for which in range(BINS):
        centre_re, centre_im = steering(centre, placed, wavenumbers[which], factor)
        centre_rows.append(jnp.concatenate([centre_re, centre_im], 1).T.astype(jnp.float32))
    count = NZ * NY

    def plane(index):
        x_value = coords_plane(index, NX)
        cells = jnp.stack([jnp.broadcast_to(x_value, (count,)), jnp.tile(y_coords, NZ), jnp.repeat(z_coords, NY)])
        beam = jnp.zeros((count,), jnp.float32)
        spread = jnp.zeros((count,), jnp.float32)
        for which in range(BINS):
            steer_re, steer_im = steering(cells, placed, wavenumbers[which], factor)
            real_f = steer_re.astype(jnp.float32)
            imag_f = steer_im.astype(jnp.float32)
            both = jnp.concatenate([real_f, imag_f], 1)
            matrix_re = csm[0, which].astype(jnp.float32)
            matrix_im = csm[1, which].astype(jnp.float32)
            first = jnp.dot(matrix_re, both, precision=highest)
            second = jnp.dot(matrix_im, imag_f, precision=highest)
            beam = beam + lax.optimization_barrier(jnp.sum(real_f * first[:, :count] + imag_f * first[:, count:] - 2.0 * real_f * second, axis=0))
            dots = jnp.dot(centre_rows[which], both, precision=highest)
            real_dot = dots[0, :count] + dots[1, count:]
            imag_dot = dots[1, :count] - dots[0, count:]
            spread = spread + (real_dot * real_dot + imag_dot * imag_dot) / BINS
        return (beam, spread)
    beams, spreads = lax.map(plane, jnp.arange(NX, dtype=jnp.int32))
    beam_map = beams.reshape(NX, NZ, NY)
    psf = spreads.reshape(NX, NZ, NY)
    kernel = jnp.roll(psf / jnp.sum(psf), (-(NX // 2), -(NZ // 2), -(NY // 2)), axis=(0, 1, 2))
    transfer = jnp.fft.fftn(kernel)
    beam_hat = jnp.fft.fftn(beam_map)
    source = jnp.zeros((NX, NZ, NY), jnp.float32)
    for sweep in range(ITERS):
        source_hat = jnp.fft.fftn(source)
        grad_hat = jnp.conj(transfer) * (transfer * source_hat - beam_hat)
        grad = jnp.real(jnp.fft.ifftn(grad_hat)).astype(jnp.float32)
        image = jnp.real(jnp.fft.ifftn(transfer * grad_hat)).astype(jnp.float32)
        length = jnp.sum(grad * grad) / (jnp.sum(image * image) + 1e-06)
        source = jnp.maximum(source - length * grad, 0.0)
    return (beam_map, source)
```

```python
import functools
import math

import jax
import jax.numpy as jnp
import numpy as np
from jax import lax
from jax.experimental import pallas as pl
from jax.experimental.pallas import tpu as pltpu
from jax.sharding import PartitionSpec as P

NY = 128
CX = 4
CZ = 4
ITERS = 3


highest = lax.Precision.HIGHEST


def coords_plane(index, length):
    return (2.0 * index.astype(jnp.float32) + 1.0) / length - 1.0


def coords_depth(index, length):
    return 2.0 + (index.astype(jnp.float32) + 0.5) / length


def steering(cells, placed, rate, factor):
    diff_x = cells[0][None, :] - placed[0][:, None]
    diff_y = cells[1][None, :] - placed[1][:, None]
    diff_z = cells[2][None, :] - placed[2][:, None]
    dist = jnp.sqrt(diff_x * diff_x + diff_y * diff_y + diff_z * diff_z)
    phase = rate * dist
    return (
        (jnp.cos(phase) * factor).astype(jnp.bfloat16),
        (-jnp.sin(phase) * factor).astype(jnp.bfloat16),
    )


def tables(length):
    counter = jnp.arange(length, dtype=jnp.int32)
    angles = (
        2.0 * math.pi / length * (counter[:, None] * counter[None, :] % length).astype(jnp.float32)
    )
    return (jnp.cos(angles), jnp.sin(angles))


def along_axis(table, values, axis):
    formula = {1: "kj,sjbc->skbc", 2: "kj,sajc->sakc", 3: "kj,sabj->sabk"}
    return jnp.einsum(formula[axis], table, values, precision=highest)


def alternate(real_part, imag_part):
    paired = jnp.stack([real_part, imag_part], 1)
    return paired.reshape((2 * real_part.shape[0],) + real_part.shape[1:])


def transform(stack, axis, sign):
    cosine, sine = tables(stack.shape[axis])
    real_part = stack[0::2]
    imag_part = stack[1::2]
    new_real = along_axis(cosine, real_part, axis) - sign * along_axis(sine, imag_part, axis)
    new_imag = along_axis(cosine, imag_part, axis) + sign * along_axis(sine, real_part, axis)
    return alternate(new_real, new_imag)


def forward(signals):
    cosine, sine = tables(signals.shape[3])
    flat = signals.reshape(-1, signals.shape[3])
    real_part = jnp.dot(flat, cosine, precision=highest).reshape(signals.shape)
    imag_part = -jnp.dot(flat, sine, precision=highest).reshape(signals.shape)
    stack = alternate(real_part, imag_part)
    stack = lax.all_to_all(stack, "gx", split_axis=3, concat_axis=1, tiled=True)
    stack = transform(stack, 1, -1.0)
    stack = lax.all_to_all(stack, ("gy", "gz"), split_axis=1, concat_axis=2, tiled=True)
    stack = transform(stack, 2, -1.0)
    return stack


def inverse(stack, total):
    stack = transform(stack, 2, 1.0)
    stack = lax.all_to_all(stack, ("gy", "gz"), split_axis=2, concat_axis=1, tiled=True)
    stack = transform(stack, 1, 1.0)
    stack = lax.all_to_all(stack, "gx", split_axis=1, concat_axis=3, tiled=True)
    cosine, sine = tables(stack.shape[3])
    values = along_axis(cosine, stack[0::2], 3) - along_axis(sine, stack[1::2], 3)
    return values / total


def parity(first, second, third):
    summed = (first[:, None, None] + second[None, :, None] + third[None, None, :]) % 2
    return 1.0 - 2.0 * summed.astype(jnp.float32)


def on_device(csm, positions, mic_order, wavenumbers):
    size_x = lax.axis_size("gx")
    size_y = lax.axis_size("gy")
    size_z = lax.axis_size("gz")
    slab_index = lax.axis_index("gx")
    outer_index = lax.axis_index("gy")
    core_index = lax.axis_index("gz")
    depth_index = outer_index * size_z + core_index
    mics = csm.shape[3]
    bins = csm.shape[1]
    grid_x = CX * size_x
    grid_z = CZ * size_y * size_z
    factor = 1.0 / math.sqrt(mics)
    placed = jnp.take(positions, mic_order, axis=1)
    centre = jnp.stack(
        [
            coords_plane(jnp.full((1,), grid_x // 2, jnp.int32), grid_x),
            coords_plane(jnp.full((1,), NY // 2, jnp.int32), NY),
            coords_depth(jnp.full((1,), grid_z // 2, jnp.int32), grid_z),
        ]
    )
    centre_rows = []
    for which in range(bins):
        centre_re, centre_im = steering(centre, placed, wavenumbers[which], factor)
        centre_rows.append(jnp.concatenate([centre_re, centre_im], 1).T)
    spectra = lax.all_gather(csm, ("gx", "gy", "gz"), axis=2, tiled=True)
    depth_count = CZ
    depth_start = depth_index * CZ
    y_coords = coords_plane(jnp.arange(NY, dtype=jnp.int32), NY)
    z_coords = coords_depth(depth_start + jnp.arange(depth_count, dtype=jnp.int32), grid_z)
    count = depth_count * NY

    def plane(local):
        x_value = coords_plane(slab_index * CX + local, grid_x)
        cells = jnp.stack(
            [
                jnp.broadcast_to(x_value, (count,)),
                jnp.tile(y_coords, depth_count),
                jnp.repeat(z_coords, NY),
            ]
        )
        beam = jnp.zeros((count,), jnp.float32)
        spread = jnp.zeros((count,), jnp.float32)
        for which in range(bins):
            steer_re, steer_im = steering(cells, placed, wavenumbers[which], factor)
            both = jnp.concatenate([steer_re, steer_im], 1)
            first = jnp.dot(spectra[0, which], both, preferred_element_type=jnp.float32)
            second = jnp.dot(spectra[1, which], steer_im, preferred_element_type=jnp.float32)
            rows_re, rows_im = (steer_re, steer_im)
            rows_re = rows_re.astype(jnp.float32)
            rows_im = rows_im.astype(jnp.float32)
            beam = beam + jnp.sum(
                rows_re * first[:, :count] + rows_im * first[:, count:] - 2.0 * rows_re * second,
                axis=0,
            )
            dots = jnp.dot(centre_rows[which], both, preferred_element_type=jnp.float32)
            real_dot = dots[0, :count] + dots[1, count:]
            imag_dot = dots[1, :count] - dots[0, count:]
            spread = spread + (real_dot * real_dot + imag_dot * imag_dot) / bins
        return (beam, spread)

    beams, spreads = lax.map(plane, jnp.arange(CX, dtype=jnp.int32))
    beam_map = beams.reshape(CX, depth_count, NY)
    psf = spreads.reshape(CX, depth_count, NY)
    psf_sum = lax.psum(jnp.sum(psf), ("gx", "gy", "gz"))
    spectrum = forward(jnp.stack([psf, beam_map]))
    x_share = grid_x // (size_y * size_z)
    y_share = NY // size_x
    signs = parity(
        depth_index * x_share + jnp.arange(x_share, dtype=jnp.int32),
        jnp.arange(grid_z, dtype=jnp.int32),
        slab_index * y_share + jnp.arange(y_share, dtype=jnp.int32),
    )
    psf_real = spectrum[0] * signs / psf_sum
    psf_imag = spectrum[1] * signs / psf_sum
    beam_real = spectrum[2]
    beam_imag = spectrum[3]
    total = float(grid_x * NY * grid_z)
    source = jnp.zeros((CX, CZ, NY), jnp.float32)
    for sweep in range(ITERS):
        if sweep == 0:
            resid_real = -beam_real
            resid_imag = -beam_imag
        else:
            source_hat = forward(source[None])
            resid_real = psf_real * source_hat[0] - psf_imag * source_hat[1] - beam_real
            resid_imag = psf_real * source_hat[1] + psf_imag * source_hat[0] - beam_imag
        grad_real = psf_real * resid_real + psf_imag * resid_imag
        grad_imag = psf_real * resid_imag - psf_imag * resid_real
        image_real = psf_real * grad_real - psf_imag * grad_imag
        image_imag = psf_real * grad_imag + psf_imag * grad_real
        spaces = inverse(jnp.stack([grad_real, grad_imag, image_real, image_imag]), total)
        grad = spaces[0]
        image = spaces[1]
        grad_norm, image_norm = lax.psum(
            (jnp.sum(grad * grad), jnp.sum(image * image)), ("gx", "gy", "gz")
        )
        length = grad_norm / (image_norm + 1e-06)
        source = jnp.maximum(source - length * grad, 0.0)
    return (beam_map, source)


BF = jnp.bfloat16
F32 = jnp.float32


def fit_coeffs():
    theta = (np.cos(np.pi * (np.arange(4000) + 0.5) / 4000) + 1.0) * 0.5 * 0.25
    turns = np.sqrt(theta)
    cos_fit = np.polynomial.chebyshev.Chebyshev.fit(theta, np.cos(2 * np.pi * turns), 5)
    sin_fit = np.polynomial.chebyshev.Chebyshev.fit(theta, np.sin(2 * np.pi * turns) / turns, 4)
    to_power = lambda fit: fit.convert(kind=np.polynomial.Polynomial).coef
    return to_power(cos_fit), to_power(sin_fit)


COS_COEF, SIN_COEF = fit_coeffs()


def horner(values, coefs):
    total = float(coefs[-1]) * values + float(coefs[-2])
    for coef in coefs[-3::-1]:
        total = total * values + float(coef)
    return total


def cos_sin(turns, factor):
    magic = float(1.5 * 2.0**23)
    rest = turns - ((turns + magic) - magic)
    square = rest * rest
    cosine = horner(square, COS_COEF * factor)
    sine = horner(square, SIN_COEF * -factor) * rest
    return cosine.astype(BF), sine.astype(BF)


def split(values):
    high = values.astype(BF)
    return high, (values - high.astype(F32)).astype(BF)


def dot(first, second):
    return jnp.dot(first, second, preferred_element_type=F32)


def grid_tables(slabs, depths):
    grid_x, grid_z = CX * slabs, CZ * depths
    rows = np.arange(grid_x * grid_z)
    device, local = rows // (CX * CZ), rows % (CX * CZ)
    at_x = device // depths * CX + local // CZ
    at_z = device % depths * CZ + local % CZ
    freq_x, freq_z = rows // grid_z, rows % grid_z
    angles = (
        -2.0 * np.pi * (freq_x[:, None] * at_x[None] / grid_x + freq_z[:, None] * at_z[None] / grid_z)
    )
    wide = np.block([[np.cos(angles), -np.sin(angles)], [np.sin(angles), np.cos(angles)]])
    lines = np.arange(NY)
    turn = -2.0 * np.pi * (lines[:, None] * lines[None] % NY) / NY
    ahead = np.concatenate([np.cos(turn), np.sin(turn)], 1)

    def halves(table):
        table = table.astype(np.float32)
        high = table.astype(jnp.bfloat16)
        low = (table - high.astype(np.float32)).astype(jnp.bfloat16)
        return high, low

    wide_high, wide_low = halves(wide)
    forth = np.concatenate([wide_high, wide_low, wide_high], 1)
    back = np.concatenate([wide_high.T, wide_low.T, wide_high.T], 1)
    y_high, y_low = halves(ahead)
    y_forth = np.concatenate([y_high, y_low, y_high], 0)
    y_back = np.concatenate([y_high.T, y_low.T, y_high.T], 0)
    return forth, back, y_forth, y_back


def triple_rows(values):
    high, low = split(values)
    return jnp.concatenate([high, high, low], 0)


def triple_lanes(values):
    high, low = split(values)
    return jnp.concatenate([high, high, low], 1)


def stage_forward(stack, count, forth, y_forth):
    lines = dot(triple_lanes(stack), y_forth[...])
    size = stack.shape[0] // count
    pieces = [
        jnp.concatenate([lines[i * size : (i + 1) * size, :NY], lines[i * size : (i + 1) * size, NY:]], 0)
        for i in range(count)
    ]
    wide = pieces[0] if count == 1 else jnp.concatenate(pieces, 1)
    out = dot(forth[...], triple_rows(wide))
    return out[:size], out[size:]


def stage_inverse(real_part, imag_part, back, y_back):
    size = real_part.shape[0]
    out = dot(back[...], triple_rows(jnp.concatenate([real_part, imag_part], 0)))
    return dot(triple_lanes(jnp.concatenate([out[:size], out[size:]], 1)), y_back[...])


def full_sum(values):
    return jnp.sum(jnp.sum(values, axis=0, keepdims=True), axis=1, keepdims=True)


def deconvolve(psf, beam, grid_z, forth, back, y_forth, y_back):
    size = psf.shape[0]
    total = float(size * NY)
    spec_re, spec_im = stage_forward(jnp.concatenate([psf, beam], 0), 2, forth, y_forth)
    row = lax.broadcasted_iota(jnp.int32, (size, NY), 0)
    lane = lax.broadcasted_iota(jnp.int32, (size, NY), 1)
    odd = (row // grid_z + row % grid_z + lane) % 2
    scale = (1.0 - 2.0 * odd.astype(F32)) / full_sum(psf)
    trans_re, trans_im = spec_re[:, :NY] * scale, spec_im[:, :NY] * scale
    beam_re, beam_im = spec_re[:, NY:], spec_im[:, NY:]
    power = trans_re * trans_re + trans_im * trans_im
    data_re = trans_re * beam_re + trans_im * beam_im
    data_im = trans_re * beam_im - trans_im * beam_re
    source = None
    for sweep in range(ITERS):
        if sweep == 0:
            grad_re, grad_im = -data_re, -data_im
        else:
            hat_re, hat_im = stage_forward(source, 1, forth, y_forth)
            grad_re = power * hat_re - data_re
            grad_im = power * hat_im - data_im
        norm = grad_re * grad_re + grad_im * grad_im
        grad_norm = full_sum(norm) / total
        image_norm = full_sum(power * norm) / total
        step = grad_norm / (image_norm + 1e-06) / total
        move = step * stage_inverse(grad_re, grad_im, back, y_back)
        source = jnp.maximum(-move if sweep == 0 else source - move, 0.0)
    return source


def prepare(order, positions, centre, rates, near_x, near_z, near_y, bins, factor, mids):
    mics = order.shape[1]
    hot = (lax.broadcasted_iota(jnp.int32, (mics, mics), 0) == order[...]).astype(F32).astype(BF)
    high, rest = split(positions[...])
    mid_full = positions[...] - high.astype(F32)
    middle = mid_full.astype(BF)
    low = (mid_full - middle.astype(F32)).astype(BF)
    placed = dot(high, hot) + dot(middle, hot) + dot(low, hot)
    columns = placed.T
    wide = (mics, NY)
    near_x[...] = jnp.broadcast_to(columns[:, 0:1], wide)
    near_z[...] = jnp.broadcast_to(columns[:, 2:3], wide)
    y_value = coords_plane(lax.broadcasted_iota(jnp.int32, wide, 1), NY)
    diff = y_value - jnp.broadcast_to(columns[:, 1:2], wide)
    near_y[...] = diff * diff
    diff_x = centre[0] - placed[0:1]
    diff_y = centre[1] - placed[1:2]
    diff_z = centre[2] - placed[2:3]
    square = diff_x * diff_x + diff_y * diff_y + diff_z * diff_z
    dist = square * lax.rsqrt(square)
    for which in range(bins):
        cosine, sine = cos_sin(dist * rates[which], factor)
        cosine, sine = cosine.astype(F32), sine.astype(F32)
        rows = jnp.concatenate(
            [
                jnp.concatenate([cosine, sine], 1),
                jnp.concatenate([sine, -cosine], 1),
                jnp.zeros((6, 2 * mics), F32),
            ],
            0,
        )
        mids[which] = rows.astype(BF)


def steer_rows(chunk, block, depth_start, slab, grid_x, grid_z, rates, near, store, bins, factor):
    near_x, near_z, near_y = near
    mics = near_x.shape[0]
    size = 64
    rows = pl.ds(pl.multiple_of(block * size, size), size)
    below = pl.ds(pl.multiple_of(mics + block * size, size), size)
    x_value = (2.0 * (slab * CX + chunk // (CZ // 2)).astype(F32) + 1.0) / grid_x - 1.0
    diff_x = x_value - near_x[rows]
    plane = diff_x * diff_x + near_y[rows]
    for half in range(2):
        depth = depth_start + chunk % (CZ // 2) * 2 + half
        z_value = 2.0 + (depth.astype(F32) + 0.5) / grid_z
        diff_z = z_value - near_z[rows]
        square = plane + diff_z * diff_z
        dist = square * lax.rsqrt(square)
        for which in range(bins):
            cosine, sine = cos_sin(dist * rates[which], factor)
            store[chunk, which, rows, half * NY : (half + 1) * NY] = cosine
            store[chunk, which, below, half * NY : (half + 1) * NY] = sine


def psf_chunk(chunk, mids, store, bins):
    spread = jnp.zeros((1, 2 * NY), F32)
    for which in range(bins):
        dots = dot(mids[which], store[chunk, which])
        spread = spread + (dots[0:1] * dots[0:1] + dots[1:2] * dots[1:2]) / bins
    return spread


def beam_chunk(chunk, spectra, store, bins):
    mics = spectra.shape[2]
    beam = jnp.zeros((1, 2 * NY), F32)
    for which in range(bins):
        steer_re = store[chunk, which, :mics]
        steer_im = store[chunk, which, mics:]
        first = dot(spectra[0, which], steer_re) + dot(spectra[1, which], steer_im)
        second = dot(spectra[0, which], steer_im)
        both = steer_re.astype(F32) * first + steer_im.astype(F32) * second
        beam = beam + jnp.sum(both, axis=0, keepdims=True)
    return beam


def put_chunk(ref, chunk, values):
    ref[pl.ds(chunk * 2, 1)] = values[:, :NY]
    ref[pl.ds(chunk * 2 + 1, 1)] = values[:, NY:]


def maps_kernel(sizes, spectra, positions, order, rates_ref, beam_ref, psf_ref, store, near_x, near_z, near_y, mids):
    size_x, size_y, size_z, bins = sizes
    grid_x, grid_z = CX * size_x, CZ * size_y * size_z
    mics = order.shape[1]
    factor = 1.0 / math.sqrt(mics)
    slab = lax.axis_index("gx")
    depth_start = (lax.axis_index("gy") * size_z + lax.axis_index("gz")) * CZ
    rates = [rates_ref[which] * (0.5 / math.pi) for which in range(bins)]
    prepare(order, positions, centre_of(grid_x, grid_z), rates, near_x, near_z, near_y, bins, factor, mids)
    near = (near_x, near_z, near_y)
    blocks = mics // 64

    def steer(i, carry):
        steer_rows(i // blocks, i % blocks, depth_start, slab, grid_x, grid_z, rates, near, store, bins, factor)
        return carry

    chunks = CX * CZ // 2
    lax.fori_loop(0, chunks * blocks, steer, 0)

    def sums(chunk, carry):
        put_chunk(psf_ref, chunk, psf_chunk(chunk, mids, store, bins))
        put_chunk(beam_ref, chunk, beam_chunk(chunk, spectra, store, bins))
        return carry

    lax.fori_loop(0, chunks, sums, 0)


def centre_of(grid_x, grid_z):
    return (
        (2.0 * (grid_x // 2) + 1.0) / grid_x - 1.0,
        (2.0 * (NY // 2) + 1.0) / NY - 1.0,
        2.0 + (grid_z // 2 + 0.5) / grid_z,
    )


def deconvolve_kernel(sizes, maps, forth, back, y_forth, y_back, out, whole):
    size_x, size_y, size_z, bins = sizes
    depths = size_y * size_z
    source = deconvolve(maps[0], maps[1], CZ * depths, forth, back, y_forth, y_back)
    whole[...] = source
    own = lax.axis_index("gx") * depths + lax.axis_index("gy") * size_z + lax.axis_index("gz")
    rows = CX * CZ
    out[...] = whole[pl.ds(pl.multiple_of(own * rows, rows), rows)]


def small_device(csm, positions, mic_order, wavenumbers):
    sizes = (lax.axis_size("gx"), lax.axis_size("gy"), lax.axis_size("gz"), csm.shape[1])
    bins, mics = csm.shape[1], csm.shape[3]
    rows = CX * CZ
    count = sizes[0] * sizes[1] * sizes[2]
    scaled = csm * jnp.array([1.0, -2.0], BF)[:, None, None, None]
    spectra = lax.all_gather(scaled, ("gx", "gy", "gz"), axis=2, tiled=True)
    vmem = pl.BlockSpec(memory_space=pltpu.VMEM)
    params = pltpu.CompilerParams(vmem_limit_bytes=48 * 1024 * 1024)
    padded = jnp.pad(positions, ((0, 5), (0, 0)))
    beam, psf = pl.pallas_call(
        functools.partial(maps_kernel, sizes),
        out_shape=[jax.ShapeDtypeStruct((rows, NY), F32)] * 2,
        in_specs=[vmem, vmem, vmem, pl.BlockSpec(memory_space=pltpu.SMEM)],
        out_specs=[vmem, vmem],
        scratch_shapes=[
            pltpu.VMEM((rows // 2, bins, 2 * mics, 2 * NY), BF),
            pltpu.VMEM((mics, NY), F32),
            pltpu.VMEM((mics, NY), F32),
            pltpu.VMEM((mics, NY), F32),
            pltpu.VMEM((bins, 8, 2 * mics), BF),
        ],
        compiler_params=params,
        name="maps",
    )(spectra, padded, mic_order[None], wavenumbers)
    maps = lax.all_gather(jnp.stack([psf, beam]), ("gx", "gy", "gz"), axis=1, tiled=True)
    tables_of = [jnp.asarray(t) for t in grid_tables(sizes[0], sizes[1] * sizes[2])]
    source = pl.pallas_call(
        functools.partial(deconvolve_kernel, sizes),
        out_shape=jax.ShapeDtypeStruct((rows, NY), F32),
        in_specs=[vmem] * 5,
        out_specs=vmem,
        scratch_shapes=[pltpu.VMEM((count * rows, NY), F32)],
        compiler_params=params,
        name="deconvolve",
    )(maps, *tables_of)
    return beam.reshape(CX, CZ, NY), source.reshape(CX, CZ, NY)


def solution(mesh):
    sizes = mesh.shape
    devices = sizes["gx"] * sizes["gy"] * sizes["gz"]
    body = small_device if devices <= 16 else on_device
    return jax.shard_map(
        body,
        mesh=mesh,
        in_specs=(P(None, "band", ("gx", "gy", "gz"), None), P(), P(), P("band")),
        out_specs=(P(("band", "gx"), ("gy", "gz"), None), P(("band", "gx"), ("gy", "gz"), None)),
        check_vma=False,
    )
```

```python
import functools
import math

import jax
import jax.numpy as jnp
import numpy as np
from jax import lax
from jax.experimental import pallas as pl
from jax.experimental.pallas import tpu as pltpu
from jax.sharding import PartitionSpec as P

NY = 128
CX = 4
CZ = 4
ITERS = 3


highest = lax.Precision.HIGHEST


def coords_plane(index, length):
    return (2.0 * index.astype(jnp.float32) + 1.0) / length - 1.0


def coords_depth(index, length):
    return 2.0 + (index.astype(jnp.float32) + 0.5) / length


def steering(cells, placed, rate, factor):
    diff_x = cells[0][None, :] - placed[0][:, None]
    diff_y = cells[1][None, :] - placed[1][:, None]
    diff_z = cells[2][None, :] - placed[2][:, None]
    dist = jnp.sqrt(diff_x * diff_x + diff_y * diff_y + diff_z * diff_z)
    phase = rate * dist
    return (
        (jnp.cos(phase) * factor).astype(jnp.bfloat16),
        (-jnp.sin(phase) * factor).astype(jnp.bfloat16),
    )


def tables(length):
    counter = jnp.arange(length, dtype=jnp.int32)
    angles = (
        2.0 * math.pi / length * (counter[:, None] * counter[None, :] % length).astype(jnp.float32)
    )
    return (jnp.cos(angles), jnp.sin(angles))


def along_axis(table, values, axis):
    formula = {1: "kj,sjbc->skbc", 2: "kj,sajc->sakc", 3: "kj,sabj->sabk"}
    return jnp.einsum(formula[axis], table, values, precision=highest)


def alternate(real_part, imag_part):
    paired = jnp.stack([real_part, imag_part], 1)
    return paired.reshape((2 * real_part.shape[0],) + real_part.shape[1:])


def transform(stack, axis, sign):
    cosine, sine = tables(stack.shape[axis])
    real_part = stack[0::2]
    imag_part = stack[1::2]
    new_real = along_axis(cosine, real_part, axis) - sign * along_axis(sine, imag_part, axis)
    new_imag = along_axis(cosine, imag_part, axis) + sign * along_axis(sine, real_part, axis)
    return alternate(new_real, new_imag)


def forward(signals):
    cosine, sine = tables(signals.shape[3])
    flat = signals.reshape(-1, signals.shape[3])
    real_part = jnp.dot(flat, cosine, precision=highest).reshape(signals.shape)
    imag_part = -jnp.dot(flat, sine, precision=highest).reshape(signals.shape)
    stack = alternate(real_part, imag_part)
    stack = lax.all_to_all(stack, "gx", split_axis=3, concat_axis=1, tiled=True)
    stack = transform(stack, 1, -1.0)
    stack = lax.all_to_all(stack, ("gy", "gz"), split_axis=1, concat_axis=2, tiled=True)
    stack = transform(stack, 2, -1.0)
    return stack


def inverse(stack, total):
    stack = transform(stack, 2, 1.0)
    stack = lax.all_to_all(stack, ("gy", "gz"), split_axis=2, concat_axis=1, tiled=True)
    stack = transform(stack, 1, 1.0)
    stack = lax.all_to_all(stack, "gx", split_axis=1, concat_axis=3, tiled=True)
    cosine, sine = tables(stack.shape[3])
    values = along_axis(cosine, stack[0::2], 3) - along_axis(sine, stack[1::2], 3)
    return values / total


def parity(first, second, third):
    summed = (first[:, None, None] + second[None, :, None] + third[None, None, :]) % 2
    return 1.0 - 2.0 * summed.astype(jnp.float32)


def on_device(csm, positions, mic_order, wavenumbers):
    size_x = lax.axis_size("gx")
    size_y = lax.axis_size("gy")
    size_z = lax.axis_size("gz")
    slab_index = lax.axis_index("gx")
    outer_index = lax.axis_index("gy")
    core_index = lax.axis_index("gz")
    depth_index = outer_index * size_z + core_index
    mics = csm.shape[3]
    bins = csm.shape[1]
    grid_x = CX * size_x
    grid_z = CZ * size_y * size_z
    factor = 1.0 / math.sqrt(mics)
    placed = jnp.take(positions, mic_order, axis=1)
    centre = jnp.stack(
        [
            coords_plane(jnp.full((1,), grid_x // 2, jnp.int32), grid_x),
            coords_plane(jnp.full((1,), NY // 2, jnp.int32), NY),
            coords_depth(jnp.full((1,), grid_z // 2, jnp.int32), grid_z),
        ]
    )
    centre_rows = []
    for which in range(bins):
        centre_re, centre_im = steering(centre, placed, wavenumbers[which], factor)
        centre_rows.append(jnp.concatenate([centre_re, centre_im], 1).T)
    spectra = lax.all_gather(csm, ("gx", "gy", "gz"), axis=2, tiled=True)
    depth_count = CZ
    depth_start = depth_index * CZ
    y_coords = coords_plane(jnp.arange(NY, dtype=jnp.int32), NY)
    z_coords = coords_depth(depth_start + jnp.arange(depth_count, dtype=jnp.int32), grid_z)
    count = depth_count * NY

    def plane(local):
        x_value = coords_plane(slab_index * CX + local, grid_x)
        cells = jnp.stack(
            [
                jnp.broadcast_to(x_value, (count,)),
                jnp.tile(y_coords, depth_count),
                jnp.repeat(z_coords, NY),
            ]
        )
        beam = jnp.zeros((count,), jnp.float32)
        spread = jnp.zeros((count,), jnp.float32)
        for which in range(bins):
            steer_re, steer_im = steering(cells, placed, wavenumbers[which], factor)
            both = jnp.concatenate([steer_re, steer_im], 1)
            first = jnp.dot(spectra[0, which], both, preferred_element_type=jnp.float32)
            second = jnp.dot(spectra[1, which], steer_im, preferred_element_type=jnp.float32)
            rows_re, rows_im = (steer_re, steer_im)
            rows_re = rows_re.astype(jnp.float32)
            rows_im = rows_im.astype(jnp.float32)
            beam = beam + jnp.sum(
                rows_re * first[:, :count] + rows_im * first[:, count:] - 2.0 * rows_re * second,
                axis=0,
            )
            dots = jnp.dot(centre_rows[which], both, preferred_element_type=jnp.float32)
            real_dot = dots[0, :count] + dots[1, count:]
            imag_dot = dots[1, :count] - dots[0, count:]
            spread = spread + (real_dot * real_dot + imag_dot * imag_dot) / bins
        return (beam, spread)

    beams, spreads = lax.map(plane, jnp.arange(CX, dtype=jnp.int32))
    beam_map = beams.reshape(CX, depth_count, NY)
    psf = spreads.reshape(CX, depth_count, NY)
    psf_sum = lax.psum(jnp.sum(psf), ("gx", "gy", "gz"))
    spectrum = forward(jnp.stack([psf, beam_map]))
    x_share = grid_x // (size_y * size_z)
    y_share = NY // size_x
    signs = parity(
        depth_index * x_share + jnp.arange(x_share, dtype=jnp.int32),
        jnp.arange(grid_z, dtype=jnp.int32),
        slab_index * y_share + jnp.arange(y_share, dtype=jnp.int32),
    )
    psf_real = spectrum[0] * signs / psf_sum
    psf_imag = spectrum[1] * signs / psf_sum
    beam_real = spectrum[2]
    beam_imag = spectrum[3]
    total = float(grid_x * NY * grid_z)
    source = jnp.zeros((CX, CZ, NY), jnp.float32)
    for sweep in range(ITERS):
        if sweep == 0:
            resid_real = -beam_real
            resid_imag = -beam_imag
        else:
            source_hat = forward(source[None])
            resid_real = psf_real * source_hat[0] - psf_imag * source_hat[1] - beam_real
            resid_imag = psf_real * source_hat[1] + psf_imag * source_hat[0] - beam_imag
        grad_real = psf_real * resid_real + psf_imag * resid_imag
        grad_imag = psf_real * resid_imag - psf_imag * resid_real
        image_real = psf_real * grad_real - psf_imag * grad_imag
        image_imag = psf_real * grad_imag + psf_imag * grad_real
        spaces = inverse(jnp.stack([grad_real, grad_imag, image_real, image_imag]), total)
        grad = spaces[0]
        image = spaces[1]
        grad_norm, image_norm = lax.psum(
            (jnp.sum(grad * grad), jnp.sum(image * image)), ("gx", "gy", "gz")
        )
        length = grad_norm / (image_norm + 1e-06)
        source = jnp.maximum(source - length * grad, 0.0)
    return (beam_map, source)


BF = jnp.bfloat16
F32 = jnp.float32


def fit_coeffs():
    theta = (np.cos(np.pi * (np.arange(4000) + 0.5) / 4000) + 1.0) * 0.5 * 0.25
    turns = np.sqrt(theta)
    cos_fit = np.polynomial.chebyshev.Chebyshev.fit(theta, np.cos(2 * np.pi * turns), 5)
    sin_fit = np.polynomial.chebyshev.Chebyshev.fit(theta, np.sin(2 * np.pi * turns) / turns, 4)
    to_power = lambda fit: fit.convert(kind=np.polynomial.Polynomial).coef
    return to_power(cos_fit), to_power(sin_fit)


COS_COEF, SIN_COEF = fit_coeffs()


def horner(values, coefs):
    total = float(coefs[-1]) * values + float(coefs[-2])
    for coef in coefs[-3::-1]:
        total = total * values + float(coef)
    return total


def cos_sin(turns, factor):
    magic = float(1.5 * 2.0**23)
    rest = turns - ((turns + magic) - magic)
    square = rest * rest
    cosine = horner(square, COS_COEF * factor)
    sine = horner(square, SIN_COEF * -factor) * rest
    return cosine.astype(BF), sine.astype(BF)


def split(values):
    high = values.astype(BF)
    return high, (values - high.astype(F32)).astype(BF)


def dot(first, second):
    return jnp.dot(first, second, preferred_element_type=F32)


def grid_tables(slabs, depths):
    grid_x, grid_z = CX * slabs, CZ * depths
    rows = np.arange(grid_x * grid_z)
    device, local = rows // (CX * CZ), rows % (CX * CZ)
    at_x = device // depths * CX + local // CZ
    at_z = device % depths * CZ + local % CZ
    freq_x, freq_z = rows // grid_z, rows % grid_z
    angles = (
        -2.0 * np.pi * (freq_x[:, None] * at_x[None] / grid_x + freq_z[:, None] * at_z[None] / grid_z)
    )
    wide = np.block([[np.cos(angles), -np.sin(angles)], [np.sin(angles), np.cos(angles)]])
    lines = np.arange(NY)
    turn = -2.0 * np.pi * (lines[:, None] * lines[None] % NY) / NY
    ahead = np.concatenate([np.cos(turn), np.sin(turn)], 1)

    def halves(table):
        table = table.astype(np.float32)
        high = table.astype(jnp.bfloat16)
        low = (table - high.astype(np.float32)).astype(jnp.bfloat16)
        return high, low

    wide_high, wide_low = halves(wide)
    forth = np.concatenate([wide_high, wide_low, wide_high], 1)
    back = np.concatenate([wide_high.T, wide_low.T, wide_high.T], 1)
    y_high, y_low = halves(ahead)
    y_forth = np.concatenate([y_high, y_low, y_high], 0)
    y_back = np.concatenate([y_high.T, y_low.T, y_high.T], 0)
    return forth, back, y_forth, y_back


def triple_rows(values):
    high, low = split(values)
    return jnp.concatenate([high, high, low], 0)


def triple_lanes(values):
    high, low = split(values)
    return jnp.concatenate([high, high, low], 1)


def stage_forward(stack, count, forth, y_forth):
    lines = dot(triple_lanes(stack), y_forth[...])
    size = stack.shape[0] // count
    pieces = [
        jnp.concatenate([lines[i * size : (i + 1) * size, :NY], lines[i * size : (i + 1) * size, NY:]], 0)
        for i in range(count)
    ]
    wide = pieces[0] if count == 1 else jnp.concatenate(pieces, 1)
    out = dot(forth[...], triple_rows(wide))
    return out[:size], out[size:]


def stage_inverse(real_part, imag_part, back, y_back):
    size = real_part.shape[0]
    out = dot(back[...], triple_rows(jnp.concatenate([real_part, imag_part], 0)))
    return dot(triple_lanes(jnp.concatenate([out[:size], out[size:]], 1)), y_back[...])


def full_sum(values):
    return jnp.sum(jnp.sum(values, axis=0, keepdims=True), axis=1, keepdims=True)


def transfer_of(psf, grid_z, forth, y_forth):
    spec_re, spec_im = stage_forward(psf, 1, forth, y_forth)
    shape = psf.shape
    row = lax.broadcasted_iota(jnp.int32, shape, 0)
    lane = lax.broadcasted_iota(jnp.int32, shape, 1)
    odd = (row // grid_z + row % grid_z + lane) % 2
    scale = (1.0 - 2.0 * odd.astype(F32)) / full_sum(psf)
    return spec_re * scale, spec_im * scale


def deconvolve(transfer, beam, forth, back, y_forth, y_back):
    total = float(beam.shape[0] * NY)
    trans_re, trans_im = transfer
    beam_re, beam_im = stage_forward(beam, 1, forth, y_forth)
    power = trans_re * trans_re + trans_im * trans_im
    data_re = trans_re * beam_re + trans_im * beam_im
    data_im = trans_re * beam_im - trans_im * beam_re
    source = None
    for sweep in range(ITERS):
        if sweep == 0:
            grad_re, grad_im = -data_re, -data_im
        else:
            hat_re, hat_im = stage_forward(source, 1, forth, y_forth)
            grad_re = power * hat_re - data_re
            grad_im = power * hat_im - data_im
        norm = grad_re * grad_re + grad_im * grad_im
        grad_norm = full_sum(norm) / total
        image_norm = full_sum(power * norm) / total
        step = grad_norm / (image_norm + 1e-06) / total
        move = step * stage_inverse(grad_re, grad_im, back, y_back)
        source = jnp.maximum(-move if sweep == 0 else source - move, 0.0)
    return source


def prepare(order, positions, centre, rates, near_x, near_z, near_y, bins, factor, mids):
    mics = order.shape[1]
    hot = (lax.broadcasted_iota(jnp.int32, (mics, mics), 0) == order[...]).astype(F32).astype(BF)
    values = jnp.concatenate([positions[...], jnp.zeros((5, mics), F32)], 0)
    high = values.astype(BF)
    mid_full = values - high.astype(F32)
    middle = mid_full.astype(BF)
    low = (mid_full - middle.astype(F32)).astype(BF)
    placed = dot(high, hot) + dot(middle, hot) + dot(low, hot)
    columns = placed.T
    wide = (mics, NY)
    near_x[...] = jnp.broadcast_to(columns[:, 0:1], wide)
    near_z[...] = jnp.broadcast_to(columns[:, 2:3], wide)
    y_value = coords_plane(lax.broadcasted_iota(jnp.int32, wide, 1), NY)
    diff = y_value - jnp.broadcast_to(columns[:, 1:2], wide)
    near_y[...] = diff * diff
    diff_x = centre[0] - placed[0:1]
    diff_y = centre[1] - placed[1:2]
    diff_z = centre[2] - placed[2:3]
    square = diff_x * diff_x + diff_y * diff_y + diff_z * diff_z
    dist = square * lax.rsqrt(square)
    for which in range(bins):
        cosine, sine = cos_sin(dist * rates[which], factor)
        cosine, sine = cosine.astype(F32), sine.astype(F32)
        rows = jnp.concatenate(
            [
                jnp.concatenate([cosine, sine], 1),
                jnp.concatenate([sine, -cosine], 1),
                jnp.zeros((6, 2 * mics), F32),
            ],
            0,
        )
        mids[which] = rows.astype(BF)


def steer_rows(chunk, block, depth_start, slab, grid_x, grid_z, rates, near, store, bins, factor):
    near_x, near_z, near_y = near
    mics = near_x.shape[0]
    size = 64
    rows = pl.ds(pl.multiple_of(block * size, size), size)
    below = pl.ds(pl.multiple_of(mics + block * size, size), size)
    x_value = (2.0 * (slab * CX + chunk // (CZ // 2)).astype(F32) + 1.0) / grid_x - 1.0
    diff_x = x_value - near_x[rows]
    plane = diff_x * diff_x + near_y[rows]
    for half in range(2):
        depth = depth_start + chunk % (CZ // 2) * 2 + half
        z_value = 2.0 + (depth.astype(F32) + 0.5) / grid_z
        diff_z = z_value - near_z[rows]
        square = plane + diff_z * diff_z
        dist = square * lax.rsqrt(square)
        for which in range(bins):
            cosine, sine = cos_sin(dist * rates[which], factor)
            store[chunk, which, rows, half * NY : (half + 1) * NY] = cosine
            store[chunk, which, below, half * NY : (half + 1) * NY] = sine


def psf_chunk(chunk, mids, store, bins):
    spread = jnp.zeros((1, 2 * NY), F32)
    for which in range(bins):
        dots = dot(mids[which], store[chunk, which])
        spread = spread + (dots[0:1] * dots[0:1] + dots[1:2] * dots[1:2]) / bins
    return spread


def beam_chunk(chunk, spectra, store, bins):
    mics = spectra.shape[2]
    beam = jnp.zeros((1, 2 * NY), F32)
    for which in range(bins):
        steer_re = store[chunk, which, :mics]
        steer_im = store[chunk, which, mics:]
        first = dot(spectra[0, which], steer_re) + dot(spectra[1, which], steer_im)
        second = dot(spectra[0, which], steer_im)
        both = steer_re.astype(F32) * first + steer_im.astype(F32) * second
        beam = beam + jnp.sum(both, axis=0, keepdims=True)
    return beam


def put_chunk(ref, chunk, values):
    ref[chunk // 2, pl.ds(chunk % 2 * 2, 1)] = values[:, :NY]
    ref[chunk // 2, pl.ds(chunk % 2 * 2 + 1, 1)] = values[:, NY:]


RIGHT, LEFT, ACROSS, SIBLING = range(4)
MESH = pl.DeviceIdType.MESH


def centre_of(grid_x, grid_z):
    return (
        (2.0 * (grid_x // 2) + 1.0) / grid_x - 1.0,
        (2.0 * (NY // 2) + 1.0) / NY - 1.0,
        2.0 + (grid_z // 2 + 0.5) / grid_z,
    )


def whole_kernel(
    sizes,
    csm,
    positions,
    order,
    rates_ref,
    forth_in,
    back_in,
    y_forth_in,
    y_back_in,
    beam_ref,
    source_ref,
    spectra,
    store,
    near_x,
    near_z,
    near_y,
    mids,
    maps,
    own_psf,
    forth,
    back,
    y_forth,
    y_back,
    result,
    table_sem,
    block_sent,
    block_got,
    map_sent,
    map_got,
):
    size_x, size_y, size_z, bins = sizes
    grid_x, grid_z = CX * size_x, CZ * size_y * size_z
    mics = order.shape[1]
    share = csm.shape[2]
    devices = size_x * size_y * size_z
    factor = 1.0 / math.sqrt(mics)
    at_x, at_y, at_z = lax.axis_index("gx"), lax.axis_index("gy"), lax.axis_index("gz")

    def number(x, y, z):
        return (x * size_y + y) * size_z + z

    own = number(at_x, at_y, at_z)
    depth_start = (at_y * size_z + at_z) * CZ

    def place(device):
        return {
            "gx": device // (size_y * size_z),
            "gy": device // size_z % size_y,
            "gz": device % size_z,
        }

    barrier = pltpu.get_barrier_semaphore()

    def greet(i, carry):
        pl.semaphore_signal(
            barrier, inc=1, device_id=place((own + i) % devices), device_id_type=MESH
        )
        return carry

    lax.fori_loop(1, devices, greet, 0)
    loads = [
        pltpu.make_async_copy(source, target, table_sem.at[i])
        for i, (source, target) in enumerate(
            [(forth_in, forth), (back_in, back), (y_forth_in, y_forth), (y_back_in, y_back)]
        )
    ]
    for load in loads:
        load.start()

    def rows_of(block):
        return pl.ds(pl.multiple_of(block * share, share), share)

    spectra[0, :, rows_of(own)] = csm[0]
    spectra[1, :, rows_of(own)] = (csm[1].astype(F32) * -2.0).astype(BF)
    pl.semaphore_wait(barrier, devices - 1)

    sends = []

    def block_copy(block, way, target):
        view = spectra.at[:, :, rows_of(block)]
        return pltpu.make_async_remote_copy(
            src_ref=view,
            dst_ref=view,
            send_sem=block_sent.at[way, block],
            recv_sem=block_got.at[block],
            device_id=target,
            device_id_type=MESH,
        )

    sibling, across = {"gz": 1 - at_z}, {"gy": 1 - at_y}

    def along(sign):
        return {"gx": at_x + sign}

    def send(valid, block, way, target):
        sends.append((valid, block, way, target))

        @pl.when(valid)
        def _():
            block_copy(block, way, target).start()

    def await_block(valid, block):
        @pl.when(valid)
        def _():
            block_copy(block, SIBLING, sibling).wait_recv()

    def inside(x):
        return (x >= 0) & (x < size_x)

    always = at_x >= 0

    for sign, way in ((1, RIGHT), (-1, LEFT)):
        send(inside(at_x + sign), own, way, along(sign))
    send(always, own, ACROSS, across)
    send(always, own, SIBLING, sibling)

    def pass_on(distance):
        for sign, way in ((1, RIGHT), (-1, LEFT)):
            source = at_x - sign * distance
            block = number(source, at_y, at_z)
            valid = inside(source)
            await_block(valid, block)
            if distance < size_x - 1:
                send(valid & inside(at_x + sign), block, way, along(sign))
            send(valid, block, ACROSS, across)
            send(valid, block, SIBLING, sibling)

    def pass_across(distance):
        for sign in (1, -1) if distance else (1,):
            source = at_x - sign * distance
            block = number(source, 1 - at_y, at_z)
            valid = inside(source)
            await_block(valid, block)
            send(valid, block, SIBLING, sibling)

    rates = [rates_ref[which] * (0.5 / math.pi) for which in range(bins)]
    prepare(
        order, positions, centre_of(grid_x, grid_z), rates, near_x, near_z, near_y, bins, factor, mids
    )
    near = (near_x, near_z, near_y)
    blocks = mics // 64

    def steer(i, carry):
        steer_rows(
            i // blocks, i % blocks, depth_start, at_x, grid_x, grid_z, rates, near, store, bins, factor
        )
        return carry

    chunks = CX * CZ // 2
    part = chunks * blocks // 4
    for stage in range(4):
        lax.fori_loop(part * stage, part * (stage + 1), steer, 0)
        if stage < 3 and stage + 1 < size_x:
            pass_on(stage + 1)
        if 0 < stage < 3 and stage - 1 < size_x:
            pass_across(stage - 1)

    rows = CX * CZ

    def psf_step(chunk, carry):
        put_chunk(own_psf, chunk, psf_chunk(chunk, mids, store, bins))
        return carry

    lax.fori_loop(0, chunks, psf_step, 0)

    def map_rows(device):
        return pl.ds(pl.multiple_of(device * rows, rows), rows)

    def map_copy(which, i, source):
        target = (own + i) % devices
        return pltpu.make_async_remote_copy(
            src_ref=maps.at[which, map_rows(source)],
            dst_ref=maps.at[which, map_rows(source)],
            send_sem=map_sent.at[which, i],
            recv_sem=map_got.at[which, source],
            device_id=place(target),
            device_id_type=MESH,
        )

    def spread_map(which, values):
        maps[which, map_rows(own)] = jnp.concatenate([values[x] for x in range(CX)], 0)

        def start(i, carry):
            map_copy(which, i, own).start()
            return carry

        lax.fori_loop(1, devices, start, 0)

    def await_map(which):
        def one(i, carry):
            map_copy(which, i, (own + i) % devices).wait_recv()
            return carry

        lax.fori_loop(1, devices, one, 0)

    spread_map(0, own_psf[...])
    for distance in range(2, size_x):
        pass_across(distance)
    for x in range(size_x):
        for y in range(size_y):
            await_block(always, number(x, y, 1 - at_z))

    def beam_step(chunk, carry):
        put_chunk(beam_ref, chunk, beam_chunk(chunk, spectra, store, bins))
        return carry

    lax.fori_loop(0, chunks, beam_step, 0)
    spread_map(1, beam_ref[...])
    for load in loads:
        load.wait()
    await_map(0)
    transfer = transfer_of(maps[0], grid_z, forth, y_forth)
    await_map(1)
    result[...] = deconvolve(transfer, maps[1], forth, back, y_forth, y_back)
    for x in range(CX):
        source_ref[x] = result[pl.ds(pl.multiple_of(own * rows, rows) + x * CZ, CZ)]

    for valid, block, way, target in sends:

        @pl.when(valid)
        def _():
            block_copy(block, way, target).wait_send()

    def sent(i, carry):
        for which in range(2):
            map_copy(which, i, own).wait_send()
        return carry

    lax.fori_loop(1, devices, sent, 0)


def small_device(csm, positions, mic_order, wavenumbers):
    sizes = (lax.axis_size("gx"), lax.axis_size("gy"), lax.axis_size("gz"), csm.shape[1])
    bins, mics = csm.shape[1], csm.shape[3]
    rows = CX * CZ
    devices = sizes[0] * sizes[1] * sizes[2]
    vmem = pl.BlockSpec(memory_space=pltpu.VMEM)
    anywhere = pl.BlockSpec(memory_space=pl.ANY)
    tables_of = [jnp.asarray(t) for t in grid_tables(sizes[0], sizes[1] * sizes[2])]
    beam, source = pl.pallas_call(
        functools.partial(whole_kernel, sizes),
        out_shape=[jax.ShapeDtypeStruct((CX, CZ, NY), F32)] * 2,
        in_specs=[vmem, vmem, vmem, pl.BlockSpec(memory_space=pltpu.SMEM)] + [anywhere] * 4,
        out_specs=[vmem, vmem],
        scratch_shapes=[
            pltpu.VMEM((2, bins, mics, mics), BF),
            pltpu.VMEM((rows // 2, bins, 2 * mics, 2 * NY), BF),
            pltpu.VMEM((mics, NY), F32),
            pltpu.VMEM((mics, NY), F32),
            pltpu.VMEM((mics, NY), F32),
            pltpu.VMEM((bins, 8, 2 * mics), BF),
            pltpu.VMEM((2, devices * rows, NY), F32),
            pltpu.VMEM((CX, CZ, NY), F32),
        ]
        + [pltpu.VMEM(t.shape, BF) for t in tables_of]
        + [
            pltpu.VMEM((devices * rows, NY), F32),
            pltpu.SemaphoreType.DMA((4,)),
            pltpu.SemaphoreType.DMA((4, devices)),
            pltpu.SemaphoreType.DMA((devices,)),
            pltpu.SemaphoreType.DMA((2, devices)),
            pltpu.SemaphoreType.DMA((2, devices)),
        ],
        compiler_params=pltpu.CompilerParams(
            vmem_limit_bytes=48 * 1024 * 1024, collective_id=0, has_side_effects=True
        ),
        name="maps_and_sources",
    )(csm, positions, mic_order[None], wavenumbers, *tables_of)
    return beam, source


def solution(mesh):
    sizes = mesh.shape
    small = sizes["gx"] <= 4 and sizes["gy"] == 2 and sizes["gz"] == 2
    return jax.shard_map(
        small_device if small else on_device,
        mesh=mesh,
        in_specs=(P(None, "band", ("gx", "gy", "gz"), None), P(), P(), P("band")),
        out_specs=(P(("band", "gx"), ("gy", "gz"), None), P(("band", "gx"), ("gy", "gz"), None)),
        check_vma=False,
    )
```

```python
import functools
import math

import jax
import jax.numpy as jnp
import numpy as np
from jax import lax
from jax.experimental import pallas as pl
from jax.experimental.pallas import tpu as pltpu
from jax.sharding import PartitionSpec as P

NY = 128
CX = 4
CZ = 4
ITERS = 3


highest = lax.Precision.HIGHEST


def coords_plane(index, length):
    return (2.0 * index.astype(jnp.float32) + 1.0) / length - 1.0


def coords_depth(index, length):
    return 2.0 + (index.astype(jnp.float32) + 0.5) / length


def steering(cells, placed, rate, factor):
    diff_x = cells[0][None, :] - placed[0][:, None]
    diff_y = cells[1][None, :] - placed[1][:, None]
    diff_z = cells[2][None, :] - placed[2][:, None]
    dist = jnp.sqrt(diff_x * diff_x + diff_y * diff_y + diff_z * diff_z)
    phase = rate * dist
    return (
        (jnp.cos(phase) * factor).astype(jnp.bfloat16),
        (-jnp.sin(phase) * factor).astype(jnp.bfloat16),
    )


def tables(length):
    counter = jnp.arange(length, dtype=jnp.int32)
    angles = (
        2.0 * math.pi / length * (counter[:, None] * counter[None, :] % length).astype(jnp.float32)
    )
    return (jnp.cos(angles), jnp.sin(angles))


def along_axis(table, values, axis):
    formula = {1: "kj,sjbc->skbc", 2: "kj,sajc->sakc", 3: "kj,sabj->sabk"}
    return jnp.einsum(formula[axis], table, values, precision=highest)


def alternate(real_part, imag_part):
    paired = jnp.stack([real_part, imag_part], 1)
    return paired.reshape((2 * real_part.shape[0],) + real_part.shape[1:])


def transform(stack, axis, sign):
    cosine, sine = tables(stack.shape[axis])
    real_part = stack[0::2]
    imag_part = stack[1::2]
    new_real = along_axis(cosine, real_part, axis) - sign * along_axis(sine, imag_part, axis)
    new_imag = along_axis(cosine, imag_part, axis) + sign * along_axis(sine, real_part, axis)
    return alternate(new_real, new_imag)


def forward(signals):
    cosine, sine = tables(signals.shape[3])
    flat = signals.reshape(-1, signals.shape[3])
    real_part = jnp.dot(flat, cosine, precision=highest).reshape(signals.shape)
    imag_part = -jnp.dot(flat, sine, precision=highest).reshape(signals.shape)
    stack = alternate(real_part, imag_part)
    stack = lax.all_to_all(stack, "gx", split_axis=3, concat_axis=1, tiled=True)
    stack = transform(stack, 1, -1.0)
    stack = lax.all_to_all(stack, ("gy", "gz"), split_axis=1, concat_axis=2, tiled=True)
    stack = transform(stack, 2, -1.0)
    return stack


def inverse(stack, total):
    stack = transform(stack, 2, 1.0)
    stack = lax.all_to_all(stack, ("gy", "gz"), split_axis=2, concat_axis=1, tiled=True)
    stack = transform(stack, 1, 1.0)
    stack = lax.all_to_all(stack, "gx", split_axis=1, concat_axis=3, tiled=True)
    cosine, sine = tables(stack.shape[3])
    values = along_axis(cosine, stack[0::2], 3) - along_axis(sine, stack[1::2], 3)
    return values / total


def parity(first, second, third):
    summed = (first[:, None, None] + second[None, :, None] + third[None, None, :]) % 2
    return 1.0 - 2.0 * summed.astype(jnp.float32)


def on_device(csm, positions, mic_order, wavenumbers):
    size_x = lax.axis_size("gx")
    size_y = lax.axis_size("gy")
    size_z = lax.axis_size("gz")
    slab_index = lax.axis_index("gx")
    outer_index = lax.axis_index("gy")
    core_index = lax.axis_index("gz")
    depth_index = outer_index * size_z + core_index
    mics = csm.shape[3]
    bins = csm.shape[1]
    grid_x = CX * size_x
    grid_z = CZ * size_y * size_z
    factor = 1.0 / math.sqrt(mics)
    placed = jnp.take(positions, mic_order, axis=1)
    centre = jnp.stack(
        [
            coords_plane(jnp.full((1,), grid_x // 2, jnp.int32), grid_x),
            coords_plane(jnp.full((1,), NY // 2, jnp.int32), NY),
            coords_depth(jnp.full((1,), grid_z // 2, jnp.int32), grid_z),
        ]
    )
    centre_rows = []
    for which in range(bins):
        centre_re, centre_im = steering(centre, placed, wavenumbers[which], factor)
        centre_rows.append(jnp.concatenate([centre_re, centre_im], 1).T)
    spectra = lax.all_gather(csm, ("gx", "gy", "gz"), axis=2, tiled=True)
    depth_count = CZ
    depth_start = depth_index * CZ
    y_coords = coords_plane(jnp.arange(NY, dtype=jnp.int32), NY)
    z_coords = coords_depth(depth_start + jnp.arange(depth_count, dtype=jnp.int32), grid_z)
    count = depth_count * NY

    def plane(local):
        x_value = coords_plane(slab_index * CX + local, grid_x)
        cells = jnp.stack(
            [
                jnp.broadcast_to(x_value, (count,)),
                jnp.tile(y_coords, depth_count),
                jnp.repeat(z_coords, NY),
            ]
        )
        beam = jnp.zeros((count,), jnp.float32)
        spread = jnp.zeros((count,), jnp.float32)
        for which in range(bins):
            steer_re, steer_im = steering(cells, placed, wavenumbers[which], factor)
            both = jnp.concatenate([steer_re, steer_im], 1)
            first = jnp.dot(spectra[0, which], both, preferred_element_type=jnp.float32)
            second = jnp.dot(spectra[1, which], steer_im, preferred_element_type=jnp.float32)
            rows_re, rows_im = (steer_re, steer_im)
            rows_re = rows_re.astype(jnp.float32)
            rows_im = rows_im.astype(jnp.float32)
            beam = beam + jnp.sum(
                rows_re * first[:, :count] + rows_im * first[:, count:] - 2.0 * rows_re * second,
                axis=0,
            )
            dots = jnp.dot(centre_rows[which], both, preferred_element_type=jnp.float32)
            real_dot = dots[0, :count] + dots[1, count:]
            imag_dot = dots[1, :count] - dots[0, count:]
            spread = spread + (real_dot * real_dot + imag_dot * imag_dot) / bins
        return (beam, spread)

    beams, spreads = lax.map(plane, jnp.arange(CX, dtype=jnp.int32))
    beam_map = beams.reshape(CX, depth_count, NY)
    psf = spreads.reshape(CX, depth_count, NY)
    psf_sum = lax.psum(jnp.sum(psf), ("gx", "gy", "gz"))
    spectrum = forward(jnp.stack([psf, beam_map]))
    x_share = grid_x // (size_y * size_z)
    y_share = NY // size_x
    signs = parity(
        depth_index * x_share + jnp.arange(x_share, dtype=jnp.int32),
        jnp.arange(grid_z, dtype=jnp.int32),
        slab_index * y_share + jnp.arange(y_share, dtype=jnp.int32),
    )
    psf_real = spectrum[0] * signs / psf_sum
    psf_imag = spectrum[1] * signs / psf_sum
    beam_real = spectrum[2]
    beam_imag = spectrum[3]
    total = float(grid_x * NY * grid_z)
    source = jnp.zeros((CX, CZ, NY), jnp.float32)
    for sweep in range(ITERS):
        if sweep == 0:
            resid_real = -beam_real
            resid_imag = -beam_imag
        else:
            source_hat = forward(source[None])
            resid_real = psf_real * source_hat[0] - psf_imag * source_hat[1] - beam_real
            resid_imag = psf_real * source_hat[1] + psf_imag * source_hat[0] - beam_imag
        grad_real = psf_real * resid_real + psf_imag * resid_imag
        grad_imag = psf_real * resid_imag - psf_imag * resid_real
        image_real = psf_real * grad_real - psf_imag * grad_imag
        image_imag = psf_real * grad_imag + psf_imag * grad_real
        spaces = inverse(jnp.stack([grad_real, grad_imag, image_real, image_imag]), total)
        grad = spaces[0]
        image = spaces[1]
        grad_norm, image_norm = lax.psum(
            (jnp.sum(grad * grad), jnp.sum(image * image)), ("gx", "gy", "gz")
        )
        length = grad_norm / (image_norm + 1e-06)
        source = jnp.maximum(source - length * grad, 0.0)
    return (beam_map, source)


BF = jnp.bfloat16
F32 = jnp.float32


def fit_coeffs():
    theta = (np.cos(np.pi * (np.arange(4000) + 0.5) / 4000) + 1.0) * 0.5 * 0.25
    turns = np.sqrt(theta)
    cos_fit = np.polynomial.chebyshev.Chebyshev.fit(theta, np.cos(2 * np.pi * turns), 5)
    sin_fit = np.polynomial.chebyshev.Chebyshev.fit(theta, np.sin(2 * np.pi * turns) / turns, 4)
    to_power = lambda fit: fit.convert(kind=np.polynomial.Polynomial).coef
    return to_power(cos_fit), to_power(sin_fit)


COS_COEF, SIN_COEF = fit_coeffs()


def horner(values, coefs):
    total = float(coefs[-1]) * values + float(coefs[-2])
    for coef in coefs[-3::-1]:
        total = total * values + float(coef)
    return total


def cos_sin_wide(turns, factor):
    magic = float(1.5 * 2.0**23)
    rest = turns - ((turns + magic) - magic)
    square = rest * rest
    return horner(square, COS_COEF * factor), horner(square, SIN_COEF * -factor) * rest


def cos_sin(turns, factor):
    cosine, sine = cos_sin_wide(turns, factor)
    return cosine.astype(BF), sine.astype(BF)


def split(values):
    high = values.astype(BF)
    return high, (values - high.astype(F32)).astype(BF)


def dot(first, second):
    return jnp.dot(first, second, preferred_element_type=F32)


def index_like(shape, axis):
    return lax.broadcasted_iota(jnp.int32, shape, axis)


def keep_halves(refs, rows, lanes, values):
    refs[0][rows, lanes], refs[1][rows, lanes] = split(values)


def build_tables(slabs, depths, forth, back, y_forth, y_back):
    grid_x, grid_z = CX * slabs, CZ * depths
    size = grid_x * grid_z
    first, second = slice(0, size), slice(size, 2 * size)
    for refs, freq_axis in ((forth, 0), (back, 1)):
        freq = index_like((size, size), freq_axis)
        cell = index_like((size, size), 1 - freq_axis)
        device, local = cell // (CX * CZ), cell % (CX * CZ)
        at_x = device // depths * CX + local // CZ
        at_z = device % depths * CZ + local % CZ
        turns = ((freq // grid_z * at_x) % grid_x).astype(F32) / grid_x
        turns = turns + ((freq % grid_z * at_z) % grid_z).astype(F32) / grid_z
        cosine, sine = cos_sin_wide(turns, 1.0)
        keep_halves(refs, first, first, cosine)
        keep_halves(refs, second, second, cosine)
        keep_halves(refs, first, second, -sine if freq_axis == 0 else sine)
        keep_halves(refs, second, first, sine if freq_axis == 0 else -sine)
    line = (NY, NY)
    turns = ((index_like(line, 0) * index_like(line, 1)) % NY).astype(F32) / NY
    cosine, sine = cos_sin_wide(turns, 1.0)
    first, second = slice(0, NY), slice(NY, 2 * NY)
    keep_halves(y_forth, first, first, cosine)
    keep_halves(y_forth, first, second, sine)
    keep_halves(y_back, first, first, cosine)
    keep_halves(y_back, second, first, sine)


def times_table(table, values):
    high, low = split(values)
    lanes = values.shape[1]
    both = dot(table[0], jnp.concatenate([high, low], 1))
    return both[:, :lanes] + both[:, lanes:] + dot(table[1], high)


def table_times(values, table):
    high, low = split(values)
    return dot(high, table[0]) + dot(low, table[0]) + dot(high, table[1])


def loaded(refs, rows=slice(None)):
    return tuple(ref[rows] for ref in refs)


def stage_forward(grid, forth, y_forth):
    lines = table_times(grid, loaded(y_forth))
    size = grid.shape[0]
    out = times_table(loaded(forth), jnp.concatenate([lines[:, :NY], lines[:, NY:]], 0))
    return out[:size], out[size:]


def stage_inverse(real_part, imag_part, table, y_back):
    out = times_table(table, jnp.concatenate([real_part, imag_part], 0))
    size = out.shape[0] // 2
    return table_times(jnp.concatenate([out[:size], out[size:]], 1), loaded(y_back))


def full_sum(values):
    return jnp.sum(jnp.sum(values, axis=0, keepdims=True), axis=1, keepdims=True)


def transfer_of(psf, grid_z, forth, y_forth):
    spec_re, spec_im = stage_forward(psf, forth, y_forth)
    shape = psf.shape
    row = lax.broadcasted_iota(jnp.int32, shape, 0)
    lane = lax.broadcasted_iota(jnp.int32, shape, 1)
    odd = (row // grid_z + row % grid_z + lane) % 2
    scale = (1.0 - 2.0 * odd.astype(F32)) / full_sum(psf)
    return spec_re * scale, spec_im * scale


def deconvolve(transfer, beam, forth, back, y_forth, y_back, whole, own_rows):
    total = float(beam.shape[0] * NY)
    trans_re, trans_im = transfer
    beam_re, beam_im = stage_forward(beam, forth, y_forth)
    power = trans_re * trans_re + trans_im * trans_im
    data_re = trans_re * beam_re + trans_im * beam_im
    data_im = trans_re * beam_im - trans_im * beam_re
    source = None
    for sweep in range(ITERS):
        if sweep == 0:
            grad_re, grad_im = -data_re, -data_im
        else:
            hat_re, hat_im = stage_forward(source, forth, y_forth)
            grad_re = power * hat_re - data_re
            grad_im = power * hat_im - data_im
        norm = grad_re * grad_re + grad_im * grad_im
        grad_norm = full_sum(norm) / total
        image_norm = full_sum(power * norm) / total
        step = grad_norm / (image_norm + 1e-06) / total
        if sweep < ITERS - 1:
            table = loaded(back)
        else:
            start, count = own_rows
            size = beam.shape[0]
            parts = [loaded(back, pl.ds(start + at, count)) for at in (0, size)]
            table = [jnp.concatenate([parts[0][half], parts[1][half]], 0) for half in range(2)]
            whole[...] = source
            source = whole[pl.ds(start, count)]
        move = step * stage_inverse(grad_re, grad_im, table, y_back)
        source = jnp.maximum(-move if sweep == 0 else source - move, 0.0)
    return source


def prepare(order, positions, centre, rates, near_x, near_z, near_y, bins, factor, mids):
    mics = order.shape[1]
    hot = (lax.broadcasted_iota(jnp.int32, (mics, mics), 0) == order[...]).astype(F32).astype(BF)
    values = jnp.concatenate([positions[...], jnp.zeros((5, mics), F32)], 0)
    high = values.astype(BF)
    mid_full = values - high.astype(F32)
    middle = mid_full.astype(BF)
    low = (mid_full - middle.astype(F32)).astype(BF)
    placed = dot(high, hot) + dot(middle, hot) + dot(low, hot)
    columns = placed.T
    wide = (mics, NY)
    near_x[...] = jnp.broadcast_to(columns[:, 0:1], wide)
    near_z[...] = jnp.broadcast_to(columns[:, 2:3], wide)
    y_value = coords_plane(lax.broadcasted_iota(jnp.int32, wide, 1), NY)
    diff = y_value - jnp.broadcast_to(columns[:, 1:2], wide)
    near_y[...] = diff * diff
    diff_x = centre[0] - placed[0:1]
    diff_y = centre[1] - placed[1:2]
    diff_z = centre[2] - placed[2:3]
    square = diff_x * diff_x + diff_y * diff_y + diff_z * diff_z
    dist = square * lax.rsqrt(square)
    for which in range(bins):
        cosine, sine = cos_sin(dist * rates[which], factor)
        cosine, sine = cosine.astype(F32), sine.astype(F32)
        rows = jnp.concatenate(
            [
                jnp.concatenate([cosine, sine], 1),
                jnp.concatenate([sine, -cosine], 1),
                jnp.zeros((6, 2 * mics), F32),
            ],
            0,
        )
        mids[which] = rows.astype(BF)


def steer_rows(chunk, block, depth_start, slab, grid_x, grid_z, rates, near, store, bins, factor):
    near_x, near_z, near_y = near
    mics = near_x.shape[0]
    size = 64
    rows = pl.ds(pl.multiple_of(block * size, size), size)
    below = pl.ds(pl.multiple_of(mics + block * size, size), size)
    x_value = (2.0 * (slab * CX + chunk // (CZ // 2)).astype(F32) + 1.0) / grid_x - 1.0
    diff_x = x_value - near_x[rows]
    plane = diff_x * diff_x + near_y[rows]
    for half in range(2):
        depth = depth_start + chunk % (CZ // 2) * 2 + half
        z_value = 2.0 + (depth.astype(F32) + 0.5) / grid_z
        diff_z = z_value - near_z[rows]
        square = plane + diff_z * diff_z
        dist = square * lax.rsqrt(square)
        for which in range(bins):
            cosine, sine = cos_sin(dist * rates[which], factor)
            store[chunk, which, rows, half * NY : (half + 1) * NY] = cosine
            store[chunk, which, below, half * NY : (half + 1) * NY] = sine


def psf_chunk(chunk, mids, store, bins):
    spread = jnp.zeros((1, 2 * NY), F32)
    for which in range(bins):
        dots = dot(mids[which], store[chunk, which])
        spread = spread + (dots[0:1] * dots[0:1] + dots[1:2] * dots[1:2]) / bins
    return spread


def beam_chunk(chunk, which, spectra, store):
    mics = spectra.shape[1]
    steer_re = store[chunk, which, :mics]
    steer_im = store[chunk, which, mics:]
    first = dot(spectra[2 * which], steer_re) + dot(spectra[2 * which + 1], steer_im)
    second = dot(spectra[2 * which], steer_im)
    both = steer_re.astype(F32) * first + steer_im.astype(F32) * second
    return jnp.sum(both, axis=0, keepdims=True)


def put_chunk(ref, chunk, values):
    ref[chunk // 2, pl.ds(chunk % 2 * 2, 1)] = values[:, :NY]
    ref[chunk // 2, pl.ds(chunk % 2 * 2 + 1, 1)] = values[:, NY:]


RIGHT, LEFT, ACROSS, SIBLING = range(4)
MESH = pl.DeviceIdType.MESH


def centre_of(grid_x, grid_z):
    return (
        (2.0 * (grid_x // 2) + 1.0) / grid_x - 1.0,
        (2.0 * (NY // 2) + 1.0) / NY - 1.0,
        2.0 + (grid_z // 2 + 0.5) / grid_z,
    )


def whole_kernel(
    sizes,
    csm_in,
    positions_in,
    order_in,
    rates_in,
    beam_ref,
    source_ref,
    csm,
    positions,
    order,
    rates_ref,
    spectra,
    store,
    near_x,
    near_z,
    near_y,
    mids,
    maps,
    own_psf,
    beam_more,
    forth_high,
    forth_low,
    back_high,
    back_low,
    y_forth_high,
    y_forth_low,
    y_back_high,
    y_back_low,
    whole,
    load_sem,
    block_sent,
    block_got,
    map_sent,
    map_got,
):
    forth, back = (forth_high, forth_low), (back_high, back_low)
    y_forth, y_back = (y_forth_high, y_forth_low), (y_back_high, y_back_low)
    size_x, size_y, size_z, bins = sizes
    grid_x, grid_z = CX * size_x, CZ * size_y * size_z
    mics = order.shape[1]
    share = csm.shape[2]
    devices = size_x * size_y * size_z
    factor = 1.0 / math.sqrt(mics)
    at_x, at_y, at_z = lax.axis_index("gx"), lax.axis_index("gy"), lax.axis_index("gz")

    def number(x, y, z):
        return (x * size_y + y) * size_z + z

    own = number(at_x, at_y, at_z)
    depth_start = (at_y * size_z + at_z) * CZ

    def place(device):
        return {
            "gx": device // (size_y * size_z),
            "gy": device // size_z % size_y,
            "gz": device % size_z,
        }

    barrier = pltpu.get_barrier_semaphore()

    def greet(i, carry):
        pl.semaphore_signal(
            barrier, inc=1, device_id=place((own + i) % devices), device_id_type=MESH
        )
        return carry

    lax.fori_loop(1, devices, greet, 0)
    loads = [
        pltpu.make_async_copy(source, target, load_sem.at[i])
        for i, (source, target) in enumerate(
            [(csm_in, csm), (positions_in, positions), (order_in, order), (rates_in, rates_ref)]
        )
    ]
    for load in loads:
        load.start()

    def rows_of(block):
        return pl.ds(pl.multiple_of(block * share, share), share)

    pieces = 2 * bins
    for load in loads:
        load.wait()
    for which in range(bins):
        spectra[2 * which, rows_of(own)] = csm[0, which]
        spectra[2 * which + 1, rows_of(own)] = (csm[1, which].astype(F32) * -2.0).astype(BF)
    pl.semaphore_wait(barrier, devices - 1)

    sends = []

    def block_copy(piece, block, way, target):
        view = spectra.at[piece, rows_of(block)]
        return pltpu.make_async_remote_copy(
            src_ref=view,
            dst_ref=view,
            send_sem=block_sent.at[way, piece, block],
            recv_sem=block_got.at[piece, block],
            device_id=target,
            device_id_type=MESH,
        )

    sibling, across = {"gz": 1 - at_z}, {"gy": 1 - at_y}

    def along(sign):
        return {"gx": at_x + sign}

    def send(valid, piece, block, way, target):
        sends.append((valid, piece, block, way, target))

        @pl.when(valid)
        def _():
            block_copy(piece, block, way, target).start()

    def await_block(valid, piece, block):
        @pl.when(valid)
        def _():
            block_copy(piece, block, SIBLING, sibling).wait_recv()

    def inside(x):
        return (x >= 0) & (x < size_x)

    always = at_x >= 0

    def pass_on(piece, distance):
        for sign, way in ((1, RIGHT), (-1, LEFT)):
            source = at_x - sign * distance
            block = number(source, at_y, at_z)
            valid = inside(source)
            if distance:
                await_block(valid, piece, block)
            if distance < size_x - 1:
                send(valid & inside(at_x + sign), piece, block, way, along(sign))
            if distance or sign == 1:
                send(valid, piece, block, ACROSS, across)
                send(valid, piece, block, SIBLING, sibling)

    def pass_across(piece, distance):
        for sign in (1, -1) if distance else (1,):
            source = at_x - sign * distance
            block = number(source, 1 - at_y, at_z)
            valid = inside(source)
            await_block(valid, piece, block)
            send(valid, piece, block, SIBLING, sibling)

    def exchange(slot):
        for piece in range(pieces):
            distance = slot - piece
            if 0 <= distance < size_x:
                pass_on(piece, distance)
            if 0 <= distance - 2 < size_x:
                pass_across(piece, distance - 2)

    exchange(0)
    rates = [rates_ref[0:1, which : which + 1] * (0.5 / math.pi) for which in range(bins)]
    prepare(
        order, positions, centre_of(grid_x, grid_z), rates, near_x, near_z, near_y, bins, factor, mids
    )
    near = (near_x, near_z, near_y)
    blocks = mics // 64
    chunks = CX * CZ // 2
    slots = max(chunks, pieces + size_x + 1)
    for slot in range(1, slots):
        if slot <= chunks:

            def steer(i, carry):
                steer_rows(
                    i // blocks, i % blocks, depth_start, at_x, grid_x, grid_z, rates, near, store, bins, factor
                )
                return carry

            lax.fori_loop(blocks * (slot - 1), blocks * slot, steer, 0)
            put_chunk(own_psf, slot - 1, psf_chunk(slot - 1, mids, store, bins))
        exchange(slot)

    rows = CX * CZ

    def map_rows(device):
        return pl.ds(pl.multiple_of(device * rows, rows), rows)

    def map_copy(which, i, source):
        target = (own + i) % devices
        return pltpu.make_async_remote_copy(
            src_ref=maps.at[which, map_rows(source)],
            dst_ref=maps.at[which, map_rows(source)],
            send_sem=map_sent.at[which, i],
            recv_sem=map_got.at[which, source],
            device_id=place(target),
            device_id_type=MESH,
        )

    def spread_map(which, values):
        maps[which, map_rows(own)] = jnp.concatenate([values[x] for x in range(CX)], 0)

        def start(i, carry):
            map_copy(which, i, own).start()
            return carry

        lax.fori_loop(1, devices, start, 0)

    def await_map(which):
        def one(i, carry):
            map_copy(which, i, (own + i) % devices).wait_recv()
            return carry

        lax.fori_loop(1, devices, one, 0)

    spread_map(0, own_psf[...])
    build_tables(size_x, size_y * size_z, forth, back, y_forth, y_back)
    for which in range(bins):
        for piece in (2 * which, 2 * which + 1):
            for x in range(size_x):
                for y in range(size_y):
                    await_block(always, piece, number(x, y, 1 - at_z))

        def beam_step(chunk, carry):
            put_chunk(beam_ref if which == 0 else beam_more, chunk, beam_chunk(chunk, which, spectra, store))
            return carry

        lax.fori_loop(0, chunks, beam_step, 0)
        if which:
            beam_ref[...] = beam_ref[...] + beam_more[...]
    spread_map(1, beam_ref[...])
    await_map(0)
    transfer = transfer_of(maps[0], grid_z, forth, y_forth)
    await_map(1)
    own_rows = (pl.multiple_of(own * rows, rows), rows)
    source = deconvolve(transfer, maps[1], forth, back, y_forth, y_back, whole, own_rows)
    for x in range(CX):
        source_ref[x] = source[x * CZ : (x + 1) * CZ]

    for valid, piece, block, way, target in sends:

        @pl.when(valid)
        def _():
            block_copy(piece, block, way, target).wait_send()

    def sent(i, carry):
        for which in range(2):
            map_copy(which, i, own).wait_send()
        return carry

    lax.fori_loop(1, devices, sent, 0)


def small_device(csm, positions, mic_order, wavenumbers):
    sizes = (lax.axis_size("gx"), lax.axis_size("gy"), lax.axis_size("gz"), csm.shape[1])
    bins, mics = csm.shape[1], csm.shape[3]
    rows = CX * CZ
    devices = sizes[0] * sizes[1] * sizes[2]
    size = devices * rows
    vmem = pl.BlockSpec(memory_space=pltpu.VMEM)
    beam, source = pl.pallas_call(
        functools.partial(whole_kernel, sizes),
        out_shape=[jax.ShapeDtypeStruct((CX, CZ, NY), F32)] * 2,
        in_specs=[pl.BlockSpec(memory_space=pltpu.HBM)] * 4,
        out_specs=[vmem, vmem],
        scratch_shapes=[
            pltpu.VMEM(csm.shape, BF),
            pltpu.VMEM(positions.shape, F32),
            pltpu.VMEM((1, mics), jnp.int32),
            pltpu.VMEM((1, bins), F32),
            pltpu.VMEM((2 * bins, mics, mics), BF),
            pltpu.VMEM((rows // 2, bins, 2 * mics, 2 * NY), BF),
            pltpu.VMEM((mics, NY), F32),
            pltpu.VMEM((mics, NY), F32),
            pltpu.VMEM((mics, NY), F32),
            pltpu.VMEM((bins, 8, 2 * mics), BF),
            pltpu.VMEM((2, size, NY), F32),
            pltpu.VMEM((CX, CZ, NY), F32),
            pltpu.VMEM((CX, CZ, NY), F32),
            pltpu.VMEM((2 * size, 2 * size), BF),
            pltpu.VMEM((2 * size, 2 * size), BF),
            pltpu.VMEM((2 * size, 2 * size), BF),
            pltpu.VMEM((2 * size, 2 * size), BF),
            pltpu.VMEM((NY, 2 * NY), BF),
            pltpu.VMEM((NY, 2 * NY), BF),
            pltpu.VMEM((2 * NY, NY), BF),
            pltpu.VMEM((2 * NY, NY), BF),
            pltpu.VMEM((size, NY), F32),
            pltpu.SemaphoreType.DMA((4,)),
            pltpu.SemaphoreType.DMA((4, 2 * bins, devices)),
            pltpu.SemaphoreType.DMA((2 * bins, devices)),
            pltpu.SemaphoreType.DMA((2, devices)),
            pltpu.SemaphoreType.DMA((2, devices)),
        ],
        compiler_params=pltpu.CompilerParams(
            vmem_limit_bytes=48 * 1024 * 1024, collective_id=0, has_side_effects=True
        ),
        name="maps_and_sources",
    )(csm, positions, mic_order[None], wavenumbers[None])
    return beam, source


def solution(mesh):
    sizes = mesh.shape
    small = sizes["gx"] <= 4 and sizes["gy"] == 2 and sizes["gz"] == 2
    return jax.shard_map(
        small_device if small else on_device,
        mesh=mesh,
        in_specs=(P(None, "band", ("gx", "gy", "gz"), None), P(), P(), P("band")),
        out_specs=(P(("band", "gx"), ("gy", "gz"), None), P(("band", "gx"), ("gy", "gz"), None)),
        check_vma=False,
    )
```

```python
import functools
import math

import jax
import jax.numpy as jnp
import numpy as np
from jax import lax
from jax.experimental import pallas as pl
from jax.experimental.pallas import tpu as pltpu
from jax.sharding import PartitionSpec as P

NY = 128
CX = 4
CZ = 4
ITERS = 3


highest = lax.Precision.HIGHEST


def coords_plane(index, length):
    return (2.0 * index.astype(jnp.float32) + 1.0) / length - 1.0


def coords_depth(index, length):
    return 2.0 + (index.astype(jnp.float32) + 0.5) / length


def steering(cells, placed, rate, factor):
    diff_x = cells[0][None, :] - placed[0][:, None]
    diff_y = cells[1][None, :] - placed[1][:, None]
    diff_z = cells[2][None, :] - placed[2][:, None]
    dist = jnp.sqrt(diff_x * diff_x + diff_y * diff_y + diff_z * diff_z)
    phase = rate * dist
    return (
        (jnp.cos(phase) * factor).astype(jnp.bfloat16),
        (-jnp.sin(phase) * factor).astype(jnp.bfloat16),
    )


def tables(length):
    counter = jnp.arange(length, dtype=jnp.int32)
    angles = (
        2.0 * math.pi / length * (counter[:, None] * counter[None, :] % length).astype(jnp.float32)
    )
    return (jnp.cos(angles), jnp.sin(angles))


def along_axis(table, values, axis):
    formula = {1: "kj,sjbc->skbc", 2: "kj,sajc->sakc", 3: "kj,sabj->sabk"}
    return jnp.einsum(formula[axis], table, values, precision=highest)


def alternate(real_part, imag_part):
    paired = jnp.stack([real_part, imag_part], 1)
    return paired.reshape((2 * real_part.shape[0],) + real_part.shape[1:])


def transform(stack, axis, sign):
    cosine, sine = tables(stack.shape[axis])
    real_part = stack[0::2]
    imag_part = stack[1::2]
    new_real = along_axis(cosine, real_part, axis) - sign * along_axis(sine, imag_part, axis)
    new_imag = along_axis(cosine, imag_part, axis) + sign * along_axis(sine, real_part, axis)
    return alternate(new_real, new_imag)


def forward(signals):
    cosine, sine = tables(signals.shape[3])
    flat = signals.reshape(-1, signals.shape[3])
    real_part = jnp.dot(flat, cosine, precision=highest).reshape(signals.shape)
    imag_part = -jnp.dot(flat, sine, precision=highest).reshape(signals.shape)
    stack = alternate(real_part, imag_part)
    stack = lax.all_to_all(stack, "gx", split_axis=3, concat_axis=1, tiled=True)
    stack = transform(stack, 1, -1.0)
    stack = lax.all_to_all(stack, ("gy", "gz"), split_axis=1, concat_axis=2, tiled=True)
    stack = transform(stack, 2, -1.0)
    return stack


def inverse(stack, total):
    stack = transform(stack, 2, 1.0)
    stack = lax.all_to_all(stack, ("gy", "gz"), split_axis=2, concat_axis=1, tiled=True)
    stack = transform(stack, 1, 1.0)
    stack = lax.all_to_all(stack, "gx", split_axis=1, concat_axis=3, tiled=True)
    cosine, sine = tables(stack.shape[3])
    values = along_axis(cosine, stack[0::2], 3) - along_axis(sine, stack[1::2], 3)
    return values / total


def parity(first, second, third):
    summed = (first[:, None, None] + second[None, :, None] + third[None, None, :]) % 2
    return 1.0 - 2.0 * summed.astype(jnp.float32)


def on_device(csm, positions, mic_order, wavenumbers):
    size_x = lax.axis_size("gx")
    size_y = lax.axis_size("gy")
    size_z = lax.axis_size("gz")
    slab_index = lax.axis_index("gx")
    outer_index = lax.axis_index("gy")
    core_index = lax.axis_index("gz")
    depth_index = outer_index * size_z + core_index
    mics = csm.shape[3]
    bins = csm.shape[1]
    grid_x = CX * size_x
    grid_z = CZ * size_y * size_z
    factor = 1.0 / math.sqrt(mics)
    placed = jnp.take(positions, mic_order, axis=1)
    centre = jnp.stack(
        [
            coords_plane(jnp.full((1,), grid_x // 2, jnp.int32), grid_x),
            coords_plane(jnp.full((1,), NY // 2, jnp.int32), NY),
            coords_depth(jnp.full((1,), grid_z // 2, jnp.int32), grid_z),
        ]
    )
    centre_rows = []
    for which in range(bins):
        centre_re, centre_im = steering(centre, placed, wavenumbers[which], factor)
        centre_rows.append(jnp.concatenate([centre_re, centre_im], 1).T)
    spectra = lax.all_gather(csm, ("gx", "gy", "gz"), axis=2, tiled=True)
    depth_count = CZ
    depth_start = depth_index * CZ
    y_coords = coords_plane(jnp.arange(NY, dtype=jnp.int32), NY)
    z_coords = coords_depth(depth_start + jnp.arange(depth_count, dtype=jnp.int32), grid_z)
    count = depth_count * NY

    def plane(local):
        x_value = coords_plane(slab_index * CX + local, grid_x)
        cells = jnp.stack(
            [
                jnp.broadcast_to(x_value, (count,)),
                jnp.tile(y_coords, depth_count),
                jnp.repeat(z_coords, NY),
            ]
        )
        beam = jnp.zeros((count,), jnp.float32)
        spread = jnp.zeros((count,), jnp.float32)
        for which in range(bins):
            steer_re, steer_im = steering(cells, placed, wavenumbers[which], factor)
            both = jnp.concatenate([steer_re, steer_im], 1)
            first = jnp.dot(spectra[0, which], both, preferred_element_type=jnp.float32)
            second = jnp.dot(spectra[1, which], steer_im, preferred_element_type=jnp.float32)
            rows_re, rows_im = (steer_re, steer_im)
            rows_re = rows_re.astype(jnp.float32)
            rows_im = rows_im.astype(jnp.float32)
            beam = beam + jnp.sum(
                rows_re * first[:, :count] + rows_im * first[:, count:] - 2.0 * rows_re * second,
                axis=0,
            )
            dots = jnp.dot(centre_rows[which], both, preferred_element_type=jnp.float32)
            real_dot = dots[0, :count] + dots[1, count:]
            imag_dot = dots[1, :count] - dots[0, count:]
            spread = spread + (real_dot * real_dot + imag_dot * imag_dot) / bins
        return (beam, spread)

    beams, spreads = lax.map(plane, jnp.arange(CX, dtype=jnp.int32))
    beam_map = beams.reshape(CX, depth_count, NY)
    psf = spreads.reshape(CX, depth_count, NY)
    psf_sum = lax.psum(jnp.sum(psf), ("gx", "gy", "gz"))
    spectrum = forward(jnp.stack([psf, beam_map]))
    x_share = grid_x // (size_y * size_z)
    y_share = NY // size_x
    signs = parity(
        depth_index * x_share + jnp.arange(x_share, dtype=jnp.int32),
        jnp.arange(grid_z, dtype=jnp.int32),
        slab_index * y_share + jnp.arange(y_share, dtype=jnp.int32),
    )
    psf_real = spectrum[0] * signs / psf_sum
    psf_imag = spectrum[1] * signs / psf_sum
    beam_real = spectrum[2]
    beam_imag = spectrum[3]
    total = float(grid_x * NY * grid_z)
    source = jnp.zeros((CX, CZ, NY), jnp.float32)
    for sweep in range(ITERS):
        if sweep == 0:
            resid_real = -beam_real
            resid_imag = -beam_imag
        else:
            source_hat = forward(source[None])
            resid_real = psf_real * source_hat[0] - psf_imag * source_hat[1] - beam_real
            resid_imag = psf_real * source_hat[1] + psf_imag * source_hat[0] - beam_imag
        grad_real = psf_real * resid_real + psf_imag * resid_imag
        grad_imag = psf_real * resid_imag - psf_imag * resid_real
        image_real = psf_real * grad_real - psf_imag * grad_imag
        image_imag = psf_real * grad_imag + psf_imag * grad_real
        spaces = inverse(jnp.stack([grad_real, grad_imag, image_real, image_imag]), total)
        grad = spaces[0]
        image = spaces[1]
        grad_norm, image_norm = lax.psum(
            (jnp.sum(grad * grad), jnp.sum(image * image)), ("gx", "gy", "gz")
        )
        length = grad_norm / (image_norm + 1e-06)
        source = jnp.maximum(source - length * grad, 0.0)
    return (beam_map, source)


BF = jnp.bfloat16
F32 = jnp.float32


def fit_coeffs():
    theta = (np.cos(np.pi * (np.arange(4000) + 0.5) / 4000) + 1.0) * 0.5 * 0.25
    turns = np.sqrt(theta)
    cos_fit = np.polynomial.chebyshev.Chebyshev.fit(theta, np.cos(2 * np.pi * turns), 5)
    sin_fit = np.polynomial.chebyshev.Chebyshev.fit(theta, np.sin(2 * np.pi * turns) / turns, 4)
    to_power = lambda fit: fit.convert(kind=np.polynomial.Polynomial).coef
    return to_power(cos_fit), to_power(sin_fit)


COS_COEF, SIN_COEF = fit_coeffs()


def horner(values, coefs):
    total = float(coefs[-1]) * values + float(coefs[-2])
    for coef in coefs[-3::-1]:
        total = total * values + float(coef)
    return total


def cos_sin_wide(turns, factor):
    magic = float(1.5 * 2.0**23)
    rest = turns - ((turns + magic) - magic)
    square = rest * rest
    return horner(square, COS_COEF * factor), horner(square, SIN_COEF * -factor) * rest


def cos_sin(turns, factor):
    cosine, sine = cos_sin_wide(turns, factor)
    return cosine.astype(BF), sine.astype(BF)


def split(values):
    high = values.astype(BF)
    return high, (values - high.astype(F32)).astype(BF)


def dot(first, second):
    return jnp.dot(first, second, preferred_element_type=F32)


def index_like(shape, axis):
    return lax.broadcasted_iota(jnp.int32, shape, axis)


def keep_halves(refs, rows, lanes, values):
    refs[0][rows, lanes], refs[1][rows, lanes] = split(values)


def build_tables(slabs, depths, forth, back, y_forth, y_back):
    grid_x, grid_z = CX * slabs, CZ * depths
    size = grid_x * grid_z
    first, second = slice(0, size), slice(size, 2 * size)
    for refs, freq_axis in ((forth, 0), (back, 1)):
        freq = index_like((size, size), freq_axis)
        cell = index_like((size, size), 1 - freq_axis)
        device, local = cell // (CX * CZ), cell % (CX * CZ)
        at_x = device // depths * CX + local // CZ
        at_z = device % depths * CZ + local % CZ
        turns = ((freq // grid_z * at_x) % grid_x).astype(F32) / grid_x
        turns = turns + ((freq % grid_z * at_z) % grid_z).astype(F32) / grid_z
        cosine, sine = cos_sin_wide(turns, 1.0)
        keep_halves(refs, first, first, cosine)
        keep_halves(refs, second, second, cosine)
        keep_halves(refs, first, second, -sine if freq_axis == 0 else sine)
        keep_halves(refs, second, first, sine if freq_axis == 0 else -sine)
    line = (NY, NY)
    turns = ((index_like(line, 0) * index_like(line, 1)) % NY).astype(F32) / NY
    cosine, sine = cos_sin_wide(turns, 1.0)
    first, second = slice(0, NY), slice(NY, 2 * NY)
    keep_halves(y_forth, first, first, cosine)
    keep_halves(y_forth, first, second, sine)
    keep_halves(y_back, first, first, cosine)
    keep_halves(y_back, second, first, sine)


def times_table(table, values):
    high, low = split(values)
    lanes = values.shape[1]
    both = dot(table[0], jnp.concatenate([high, low], 1))
    return both[:, :lanes] + both[:, lanes:] + dot(table[1], high)


def table_times(values, table):
    high, low = split(values)
    return dot(high, table[0]) + dot(low, table[0]) + dot(high, table[1])


def loaded(refs, rows=slice(None)):
    return tuple(ref[rows] for ref in refs)


def stage_forward(grid, forth, y_forth):
    lines = table_times(grid, loaded(y_forth))
    size = grid.shape[0]
    out = times_table(loaded(forth), jnp.concatenate([lines[:, :NY], lines[:, NY:]], 0))
    return out[:size], out[size:]


def stage_inverse(real_part, imag_part, table, y_back):
    out = times_table(table, jnp.concatenate([real_part, imag_part], 0))
    size = out.shape[0] // 2
    return table_times(jnp.concatenate([out[:size], out[size:]], 1), loaded(y_back))


def full_sum(values):
    return jnp.sum(jnp.sum(values, axis=0, keepdims=True), axis=1, keepdims=True)


def transfers_of(psf, beam, grid_z, forth, y_forth):
    size = psf.shape[0]
    lines = table_times(jnp.concatenate([psf, beam], 0), loaded(y_forth))
    grids = [
        jnp.concatenate([part[:, :NY], part[:, NY:]], 0) for part in (lines[:size], lines[size:])
    ]
    out = times_table(loaded(forth), jnp.concatenate(grids, 1))
    row, lane = index_like(psf.shape, 0), index_like(psf.shape, 1)
    odd = (row // grid_z + row % grid_z + lane) % 2
    scale = (1.0 - 2.0 * odd.astype(F32)) / full_sum(psf)
    transfer = (out[:size, :NY] * scale, out[size:, :NY] * scale)
    return transfer, (out[:size, NY:], out[size:, NY:])


def deconvolve(transfer, beam_hat, forth, back, y_forth, y_back, whole, own_rows):
    trans_re, trans_im = transfer
    beam_re, beam_im = beam_hat
    size = beam_re.shape[0]
    total = float(size * NY)
    power = trans_re * trans_re + trans_im * trans_im
    data_re = trans_re * beam_re + trans_im * beam_im
    data_im = trans_re * beam_im - trans_im * beam_re
    source = None
    for sweep in range(ITERS):
        if sweep == 0:
            grad_re, grad_im = -data_re, -data_im
        else:
            hat_re, hat_im = stage_forward(source, forth, y_forth)
            grad_re = power * hat_re - data_re
            grad_im = power * hat_im - data_im
        norm = grad_re * grad_re + grad_im * grad_im
        grad_norm = full_sum(norm) / total
        image_norm = full_sum(power * norm) / total
        step = grad_norm / (image_norm + 1e-06) / total
        if sweep < ITERS - 1:
            table = loaded(back)
        else:
            start, count = own_rows
            parts = [loaded(back, pl.ds(start + at, count)) for at in (0, size)]
            table = [jnp.concatenate([parts[0][half], parts[1][half]], 0) for half in range(2)]
            whole[...] = source
            source = whole[pl.ds(start, count)]
        move = step * stage_inverse(grad_re, grad_im, table, y_back)
        source = jnp.maximum(-move if sweep == 0 else source - move, 0.0)
    return source


def prepare(order, positions, centre, rates, near_x, near_z, near_y, bins, factor, spectra):
    mics = order.shape[1]
    hot = (lax.broadcasted_iota(jnp.int32, (mics, mics), 0) == order[...]).astype(F32).astype(BF)
    values = jnp.concatenate([positions[...], jnp.zeros((5, mics), F32)], 0)
    high = values.astype(BF)
    mid_full = values - high.astype(F32)
    middle = mid_full.astype(BF)
    low = (mid_full - middle.astype(F32)).astype(BF)
    placed = dot(high, hot) + dot(middle, hot) + dot(low, hot)
    columns = placed.T
    wide = (mics, NY)
    near_x[...] = jnp.broadcast_to(columns[:, 0:1], wide)
    near_z[...] = jnp.broadcast_to(columns[:, 2:3], wide)
    y_value = coords_plane(lax.broadcasted_iota(jnp.int32, wide, 1), NY)
    diff = y_value - jnp.broadcast_to(columns[:, 1:2], wide)
    near_y[...] = diff * diff
    diff_x = centre[0] - placed[0:1]
    diff_y = centre[1] - placed[1:2]
    diff_z = centre[2] - placed[2:3]
    square = diff_x * diff_x + diff_y * diff_y + diff_z * diff_z
    dist = square * lax.rsqrt(square)
    for which in range(bins):
        cosine, sine = cos_sin(dist * rates[which], factor)
        rows = [cosine.astype(F32), sine.astype(F32), jnp.zeros((14, mics), F32)]
        spectra[2 * which, pl.ds(mics, 16)] = jnp.concatenate(rows, 0).astype(BF)


def steer_rows(chunk, block, depth_start, slab, grid_x, grid_z, rates, near, store, bins, factor):
    near_x, near_z, near_y = near
    mics = near_x.shape[0]
    size = 64
    rows = pl.ds(pl.multiple_of(block * size, size), size)
    below = pl.ds(pl.multiple_of(mics + block * size, size), size)
    x_value = (2.0 * (slab * CX + chunk // (CZ // 2)).astype(F32) + 1.0) / grid_x - 1.0
    diff_x = x_value - near_x[rows]
    plane = diff_x * diff_x + near_y[rows]
    for half in range(2):
        depth = depth_start + chunk % (CZ // 2) * 2 + half
        z_value = 2.0 + (depth.astype(F32) + 0.5) / grid_z
        diff_z = z_value - near_z[rows]
        square = plane + diff_z * diff_z
        dist = square * lax.rsqrt(square)
        for which in range(bins):
            cosine, sine = cos_sin(dist * rates[which], factor)
            store[chunk, which, rows, half * NY : (half + 1) * NY] = cosine
            store[chunk, which, below, half * NY : (half + 1) * NY] = sine


def map_chunk(chunk, which, spectra, store, bins):
    mics = spectra.shape[2]
    steer_re = store[chunk, which, :mics]
    steer_im = store[chunk, which, mics:]
    by_re = dot(spectra[2 * which], steer_re)
    by_im = dot(spectra[2 * which], steer_im)
    first = by_re[:mics] + dot(spectra[2 * which + 1, :mics], steer_im)
    both = steer_re.astype(F32) * first + steer_im.astype(F32) * by_im[:mics]
    real_dot = by_re[mics : mics + 1] + by_im[mics + 1 : mics + 2]
    imag_dot = by_re[mics + 1 : mics + 2] - by_im[mics : mics + 1]
    spread = (real_dot * real_dot + imag_dot * imag_dot) / bins
    return jnp.sum(both, axis=0, keepdims=True), spread


def put_chunk(ref, chunk, values):
    ref[chunk // 2, pl.ds(chunk % 2 * 2, 1)] = values[:, :NY]
    ref[chunk // 2, pl.ds(chunk % 2 * 2 + 1, 1)] = values[:, NY:]


RIGHT, LEFT, ACROSS, SIBLING = range(4)
MESH = pl.DeviceIdType.MESH


def centre_of(grid_x, grid_z):
    return (
        (2.0 * (grid_x // 2) + 1.0) / grid_x - 1.0,
        (2.0 * (NY // 2) + 1.0) / NY - 1.0,
        2.0 + (grid_z // 2 + 0.5) / grid_z,
    )


def whole_kernel(
    sizes,
    csm_in,
    positions_in,
    order_in,
    rates_in,
    beam_ref,
    source_ref,
    csm,
    positions,
    order,
    rates_ref,
    spectra,
    store,
    near_x,
    near_z,
    near_y,
    maps,
    parts,
    forth_high,
    forth_low,
    back_high,
    back_low,
    y_forth_high,
    y_forth_low,
    y_back_high,
    y_back_low,
    whole,
    load_sem,
    block_sent,
    block_got,
    map_sent,
    map_got,
):
    forth, back = (forth_high, forth_low), (back_high, back_low)
    y_forth, y_back = (y_forth_high, y_forth_low), (y_back_high, y_back_low)
    size_x, size_y, size_z, bins = sizes
    grid_x, grid_z = CX * size_x, CZ * size_y * size_z
    mics = order.shape[1]
    share = csm.shape[2]
    devices = size_x * size_y * size_z
    factor = 1.0 / math.sqrt(mics)
    at_x, at_y, at_z = lax.axis_index("gx"), lax.axis_index("gy"), lax.axis_index("gz")

    def number(x, y, z):
        return (x * size_y + y) * size_z + z

    own = number(at_x, at_y, at_z)
    depth_start = (at_y * size_z + at_z) * CZ

    def place(device):
        return {
            "gx": device // (size_y * size_z),
            "gy": device // size_z % size_y,
            "gz": device % size_z,
        }

    barrier = pltpu.get_barrier_semaphore()

    def greet(i, carry):
        pl.semaphore_signal(
            barrier, inc=1, device_id=place((own + i) % devices), device_id_type=MESH
        )
        return carry

    lax.fori_loop(1, devices, greet, 0)
    loads = [
        pltpu.make_async_copy(source, target, load_sem.at[i])
        for i, (source, target) in enumerate(
            [(csm_in, csm), (positions_in, positions), (order_in, order), (rates_in, rates_ref)]
        )
    ]
    for load in loads:
        load.start()

    def rows_of(block):
        return pl.ds(pl.multiple_of(block * share, share), share)

    pieces = 2 * bins
    for load in loads:
        load.wait()
    for which in range(bins):
        spectra[2 * which, rows_of(own)] = csm[0, which]
        spectra[2 * which + 1, rows_of(own)] = (csm[1, which].astype(F32) * -2.0).astype(BF)
    pl.semaphore_wait(barrier, devices - 1)

    sends = []

    def block_copy(piece, block, way, target):
        view = spectra.at[piece, rows_of(block)]
        return pltpu.make_async_remote_copy(
            src_ref=view,
            dst_ref=view,
            send_sem=block_sent.at[way, piece, block],
            recv_sem=block_got.at[piece, block],
            device_id=target,
            device_id_type=MESH,
        )

    sibling, across = {"gz": 1 - at_z}, {"gy": 1 - at_y}

    def along(sign):
        return {"gx": at_x + sign}

    def send(valid, piece, block, way, target):
        sends.append((valid, piece, block, way, target))

        @pl.when(valid)
        def _():
            block_copy(piece, block, way, target).start()

    def await_block(valid, piece, block):
        @pl.when(valid)
        def _():
            block_copy(piece, block, SIBLING, sibling).wait_recv()

    def inside(x):
        return (x >= 0) & (x < size_x)

    always = at_x >= 0

    def from_line(piece, distance):
        for sign, way in ((1, RIGHT), (-1, LEFT)):
            source = at_x - sign * distance
            block = number(source, at_y, at_z)
            valid = inside(source)
            await_block(valid, piece, block)
            if distance < size_x - 1:
                send(valid & inside(at_x + sign), piece, block, way, along(sign))
            send(valid, piece, block, ACROSS, across)
            send(valid, piece, block, SIBLING, sibling)

    def from_across(piece, distance):
        for sign in (1, -1) if distance else (1,):
            source = at_x - sign * distance
            block = number(source, 1 - at_y, at_z)
            valid = inside(source)
            await_block(valid, piece, block)
            send(valid, piece, block, SIBLING, sibling)

    events = []
    for piece in range(pieces):
        for distance in range(size_x):
            if distance:
                events.append((1.65 * distance + 0.65 * piece, from_line, piece, distance))
            events.append((1.65 + 2.6 * distance + 0.65 * piece, from_across, piece, distance))
    events.sort(key=lambda event: event[0])

    for piece in range(pieces):
        for sign, way in ((1, RIGHT), (-1, LEFT)):
            send(inside(at_x + sign), piece, own, way, along(sign))
        send(always, piece, own, ACROSS, across)
        send(always, piece, own, SIBLING, sibling)
    rates = [rates_ref[0:1, which : which + 1] * (0.5 / math.pi) for which in range(bins)]
    prepare(
        order, positions, centre_of(grid_x, grid_z), rates, near_x, near_z, near_y, bins, factor, spectra
    )
    near = (near_x, near_z, near_y)
    blocks = mics // 64
    chunks = CX * CZ // 2
    count = chunks * blocks
    step = 4

    def steer(i, carry):
        steer_rows(
            i // blocks, i % blocks, depth_start, at_x, grid_x, grid_z, rates, near, store, bins, factor
        )
        return carry

    done = 0
    for start in range(0, count, step):
        lax.fori_loop(start, start + step, steer, 0)
        while done < len(events) * (start + step) // (count + 3 * step):
            events[done][1](*events[done][2:])
            done += 1
    build_tables(size_x, size_y * size_z, forth, back, y_forth, y_back)
    for event in events[done:]:
        event[1](*event[2:])

    rows = CX * CZ

    for which in range(bins):
        for piece in (2 * which, 2 * which + 1):
            for x in range(size_x):
                for y in range(size_y):
                    await_block(always, piece, number(x, y, 1 - at_z))

        def map_step(chunk, carry):
            beam, spread = map_chunk(chunk, which, spectra, store, bins)
            put_chunk(parts.at[which, 0], chunk, beam)
            put_chunk(parts.at[which, 1], chunk, spread)
            return carry

        lax.fori_loop(0, chunks, map_step, 0)
    for kind in range(2):
        total = parts[0, kind]
        for which in range(1, bins):
            total = total + parts[which, kind]
        maps[own, kind] = jnp.concatenate([total[x] for x in range(CX)], 0).astype(BF)
        if kind == 0:
            beam_ref[...] = total

    def map_copy(i, source):
        return pltpu.make_async_remote_copy(
            src_ref=maps.at[source],
            dst_ref=maps.at[source],
            send_sem=map_sent.at[i],
            recv_sem=map_got.at[source],
            device_id=place((own + i) % devices),
            device_id_type=MESH,
        )

    def spread_map(i, carry):
        map_copy(i, own).start()
        return carry

    def await_map(i, carry):
        map_copy(i, (own + i) % devices).wait_recv()
        return carry

    lax.fori_loop(1, devices, spread_map, 0)
    lax.fori_loop(1, devices, await_map, 0)
    size = devices * rows
    beam = maps[:, 0].reshape(size, NY).astype(F32)
    psf = maps[:, 1].reshape(size, NY).astype(F32)
    transfer, beam_hat = transfers_of(psf, beam, grid_z, forth, y_forth)
    own_rows = (pl.multiple_of(own * rows, rows), rows)
    source = deconvolve(transfer, beam_hat, forth, back, y_forth, y_back, whole, own_rows)
    for x in range(CX):
        source_ref[x] = source[x * CZ : (x + 1) * CZ]

    for valid, piece, block, way, target in sends:

        @pl.when(valid)
        def _():
            block_copy(piece, block, way, target).wait_send()

    def sent(i, carry):
        map_copy(i, own).wait_send()
        return carry

    lax.fori_loop(1, devices, sent, 0)


def small_device(csm, positions, mic_order, wavenumbers):
    sizes = (lax.axis_size("gx"), lax.axis_size("gy"), lax.axis_size("gz"), csm.shape[1])
    bins, mics = csm.shape[1], csm.shape[3]
    rows = CX * CZ
    devices = sizes[0] * sizes[1] * sizes[2]
    size = devices * rows
    vmem = pl.BlockSpec(memory_space=pltpu.VMEM)
    beam, source = pl.pallas_call(
        functools.partial(whole_kernel, sizes),
        out_shape=[jax.ShapeDtypeStruct((CX, CZ, NY), F32)] * 2,
        in_specs=[pl.BlockSpec(memory_space=pltpu.HBM)] * 4,
        out_specs=[vmem, vmem],
        scratch_shapes=[
            pltpu.VMEM(csm.shape, BF),
            pltpu.VMEM(positions.shape, F32),
            pltpu.VMEM((1, mics), jnp.int32),
            pltpu.VMEM((1, bins), F32),
            pltpu.VMEM((2 * bins, mics + 16, mics), BF),
            pltpu.VMEM((rows // 2, bins, 2 * mics, 2 * NY), BF),
            pltpu.VMEM((mics, NY), F32),
            pltpu.VMEM((mics, NY), F32),
            pltpu.VMEM((mics, NY), F32),
            pltpu.VMEM((devices, 2, rows, NY), BF),
            pltpu.VMEM((bins, 2, CX, CZ, NY), F32),
            pltpu.VMEM((2 * size, 2 * size), BF),
            pltpu.VMEM((2 * size, 2 * size), BF),
            pltpu.VMEM((2 * size, 2 * size), BF),
            pltpu.VMEM((2 * size, 2 * size), BF),
            pltpu.VMEM((NY, 2 * NY), BF),
            pltpu.VMEM((NY, 2 * NY), BF),
            pltpu.VMEM((2 * NY, NY), BF),
            pltpu.VMEM((2 * NY, NY), BF),
            pltpu.VMEM((size, NY), F32),
            pltpu.SemaphoreType.DMA((4,)),
            pltpu.SemaphoreType.DMA((4, 2 * bins, devices)),
            pltpu.SemaphoreType.DMA((2 * bins, devices)),
            pltpu.SemaphoreType.DMA((devices,)),
            pltpu.SemaphoreType.DMA((devices,)),
        ],
        compiler_params=pltpu.CompilerParams(
            vmem_limit_bytes=60 * 1024 * 1024, collective_id=0, has_side_effects=True
        ),
        name="maps_and_sources",
    )(csm, positions, mic_order[None], wavenumbers[None])
    return beam, source


def solution(mesh):
    sizes = mesh.shape
    small = sizes["gx"] <= 4 and sizes["gy"] == 2 and sizes["gz"] == 2
    return jax.shard_map(
        small_device if small else on_device,
        mesh=mesh,
        in_specs=(P(None, "band", ("gx", "gy", "gz"), None), P(), P(), P("band")),
        out_specs=(P(("band", "gx"), ("gy", "gz"), None), P(("band", "gx"), ("gy", "gz"), None)),
        check_vma=False,
    )
```

```python
import functools
import math

import jax
import jax.numpy as jnp
import numpy as np
from jax import lax
from jax.experimental import pallas as pl
from jax.experimental.pallas import tpu as pltpu
from jax.sharding import PartitionSpec as P

NY = 128
CX = 4
CZ = 4
ITERS = 3


highest = lax.Precision.HIGHEST


def coords_plane(index, length):
    return (2.0 * index.astype(jnp.float32) + 1.0) / length - 1.0


def coords_depth(index, length):
    return 2.0 + (index.astype(jnp.float32) + 0.5) / length


def steering(cells, placed, rate, factor):
    diff_x = cells[0][None, :] - placed[0][:, None]
    diff_y = cells[1][None, :] - placed[1][:, None]
    diff_z = cells[2][None, :] - placed[2][:, None]
    dist = jnp.sqrt(diff_x * diff_x + diff_y * diff_y + diff_z * diff_z)
    phase = rate * dist
    return (
        (jnp.cos(phase) * factor).astype(jnp.bfloat16),
        (-jnp.sin(phase) * factor).astype(jnp.bfloat16),
    )


def tables(length):
    counter = jnp.arange(length, dtype=jnp.int32)
    angles = (
        2.0 * math.pi / length * (counter[:, None] * counter[None, :] % length).astype(jnp.float32)
    )
    return (jnp.cos(angles), jnp.sin(angles))


def along_axis(table, values, axis):
    formula = {1: "kj,sjbc->skbc", 2: "kj,sajc->sakc", 3: "kj,sabj->sabk"}
    return jnp.einsum(formula[axis], table, values, precision=highest)


def alternate(real_part, imag_part):
    paired = jnp.stack([real_part, imag_part], 1)
    return paired.reshape((2 * real_part.shape[0],) + real_part.shape[1:])


def transform(stack, axis, sign):
    cosine, sine = tables(stack.shape[axis])
    real_part = stack[0::2]
    imag_part = stack[1::2]
    new_real = along_axis(cosine, real_part, axis) - sign * along_axis(sine, imag_part, axis)
    new_imag = along_axis(cosine, imag_part, axis) + sign * along_axis(sine, real_part, axis)
    return alternate(new_real, new_imag)


def forward(signals):
    cosine, sine = tables(signals.shape[3])
    flat = signals.reshape(-1, signals.shape[3])
    real_part = jnp.dot(flat, cosine, precision=highest).reshape(signals.shape)
    imag_part = -jnp.dot(flat, sine, precision=highest).reshape(signals.shape)
    stack = alternate(real_part, imag_part)
    stack = lax.all_to_all(stack, "gx", split_axis=3, concat_axis=1, tiled=True)
    stack = transform(stack, 1, -1.0)
    stack = lax.all_to_all(stack, ("gy", "gz"), split_axis=1, concat_axis=2, tiled=True)
    stack = transform(stack, 2, -1.0)
    return stack


def inverse(stack, total):
    stack = transform(stack, 2, 1.0)
    stack = lax.all_to_all(stack, ("gy", "gz"), split_axis=2, concat_axis=1, tiled=True)
    stack = transform(stack, 1, 1.0)
    stack = lax.all_to_all(stack, "gx", split_axis=1, concat_axis=3, tiled=True)
    cosine, sine = tables(stack.shape[3])
    values = along_axis(cosine, stack[0::2], 3) - along_axis(sine, stack[1::2], 3)
    return values / total


def parity(first, second, third):
    summed = (first[:, None, None] + second[None, :, None] + third[None, None, :]) % 2
    return 1.0 - 2.0 * summed.astype(jnp.float32)


def on_device(csm, positions, mic_order, wavenumbers):
    size_x = lax.axis_size("gx")
    size_y = lax.axis_size("gy")
    size_z = lax.axis_size("gz")
    slab_index = lax.axis_index("gx")
    outer_index = lax.axis_index("gy")
    core_index = lax.axis_index("gz")
    depth_index = outer_index * size_z + core_index
    mics = csm.shape[3]
    bins = csm.shape[1]
    grid_x = CX * size_x
    grid_z = CZ * size_y * size_z
    factor = 1.0 / math.sqrt(mics)
    placed = jnp.take(positions, mic_order, axis=1)
    centre = jnp.stack(
        [
            coords_plane(jnp.full((1,), grid_x // 2, jnp.int32), grid_x),
            coords_plane(jnp.full((1,), NY // 2, jnp.int32), NY),
            coords_depth(jnp.full((1,), grid_z // 2, jnp.int32), grid_z),
        ]
    )
    centre_rows = []
    for which in range(bins):
        centre_re, centre_im = steering(centre, placed, wavenumbers[which], factor)
        centre_rows.append(jnp.concatenate([centre_re, centre_im], 1).T)
    spectra = lax.all_gather(csm, ("gx", "gy", "gz"), axis=2, tiled=True)
    depth_count = CZ
    depth_start = depth_index * CZ
    y_coords = coords_plane(jnp.arange(NY, dtype=jnp.int32), NY)
    z_coords = coords_depth(depth_start + jnp.arange(depth_count, dtype=jnp.int32), grid_z)
    count = depth_count * NY

    def plane(local):
        x_value = coords_plane(slab_index * CX + local, grid_x)
        cells = jnp.stack(
            [
                jnp.broadcast_to(x_value, (count,)),
                jnp.tile(y_coords, depth_count),
                jnp.repeat(z_coords, NY),
            ]
        )
        beam = jnp.zeros((count,), jnp.float32)
        spread = jnp.zeros((count,), jnp.float32)
        for which in range(bins):
            steer_re, steer_im = steering(cells, placed, wavenumbers[which], factor)
            both = jnp.concatenate([steer_re, steer_im], 1)
            first = jnp.dot(spectra[0, which], both, preferred_element_type=jnp.float32)
            second = jnp.dot(spectra[1, which], steer_im, preferred_element_type=jnp.float32)
            rows_re, rows_im = (steer_re, steer_im)
            rows_re = rows_re.astype(jnp.float32)
            rows_im = rows_im.astype(jnp.float32)
            beam = beam + jnp.sum(
                rows_re * first[:, :count] + rows_im * first[:, count:] - 2.0 * rows_re * second,
                axis=0,
            )
            dots = jnp.dot(centre_rows[which], both, preferred_element_type=jnp.float32)
            real_dot = dots[0, :count] + dots[1, count:]
            imag_dot = dots[1, :count] - dots[0, count:]
            spread = spread + (real_dot * real_dot + imag_dot * imag_dot) / bins
        return (beam, spread)

    beams, spreads = lax.map(plane, jnp.arange(CX, dtype=jnp.int32))
    beam_map = beams.reshape(CX, depth_count, NY)
    psf = spreads.reshape(CX, depth_count, NY)
    psf_sum = lax.psum(jnp.sum(psf), ("gx", "gy", "gz"))
    spectrum = forward(jnp.stack([psf, beam_map]))
    x_share = grid_x // (size_y * size_z)
    y_share = NY // size_x
    signs = parity(
        depth_index * x_share + jnp.arange(x_share, dtype=jnp.int32),
        jnp.arange(grid_z, dtype=jnp.int32),
        slab_index * y_share + jnp.arange(y_share, dtype=jnp.int32),
    )
    psf_real = spectrum[0] * signs / psf_sum
    psf_imag = spectrum[1] * signs / psf_sum
    beam_real = spectrum[2]
    beam_imag = spectrum[3]
    total = float(grid_x * NY * grid_z)
    source = jnp.zeros((CX, CZ, NY), jnp.float32)
    for sweep in range(ITERS):
        if sweep == 0:
            resid_real = -beam_real
            resid_imag = -beam_imag
        else:
            source_hat = forward(source[None])
            resid_real = psf_real * source_hat[0] - psf_imag * source_hat[1] - beam_real
            resid_imag = psf_real * source_hat[1] + psf_imag * source_hat[0] - beam_imag
        grad_real = psf_real * resid_real + psf_imag * resid_imag
        grad_imag = psf_real * resid_imag - psf_imag * resid_real
        image_real = psf_real * grad_real - psf_imag * grad_imag
        image_imag = psf_real * grad_imag + psf_imag * grad_real
        spaces = inverse(jnp.stack([grad_real, grad_imag, image_real, image_imag]), total)
        grad = spaces[0]
        image = spaces[1]
        grad_norm, image_norm = lax.psum(
            (jnp.sum(grad * grad), jnp.sum(image * image)), ("gx", "gy", "gz")
        )
        length = grad_norm / (image_norm + 1e-06)
        source = jnp.maximum(source - length * grad, 0.0)
    return (beam_map, source)


BF = jnp.bfloat16
F32 = jnp.float32


def fit_coeffs():
    theta = (np.cos(np.pi * (np.arange(4000) + 0.5) / 4000) + 1.0) * 0.5 * 0.25
    turns = np.sqrt(theta)
    cos_fit = np.polynomial.chebyshev.Chebyshev.fit(theta, np.cos(2 * np.pi * turns), 5)
    sin_fit = np.polynomial.chebyshev.Chebyshev.fit(theta, np.sin(2 * np.pi * turns) / turns, 4)
    to_power = lambda fit: fit.convert(kind=np.polynomial.Polynomial).coef
    return to_power(cos_fit), to_power(sin_fit)


COS_COEF, SIN_COEF = fit_coeffs()


def horner(values, coefs):
    total = float(coefs[-1]) * values + float(coefs[-2])
    for coef in coefs[-3::-1]:
        total = total * values + float(coef)
    return total


def cos_sin_wide(turns, factor):
    magic = float(1.5 * 2.0**23)
    rest = turns - ((turns + magic) - magic)
    square = rest * rest
    return horner(square, COS_COEF * factor), horner(square, SIN_COEF * -factor) * rest


def cos_sin(turns, factor):
    cosine, sine = cos_sin_wide(turns, factor)
    return cosine.astype(BF), sine.astype(BF)


def split(values):
    high = values.astype(BF)
    return high, (values - high.astype(F32)).astype(BF)


def dot(first, second):
    return jnp.dot(first, second, preferred_element_type=F32)


def index_like(shape, axis):
    return lax.broadcasted_iota(jnp.int32, shape, axis)


def keep_halves(refs, rows, lanes, values):
    refs[0][rows, lanes], refs[1][rows, lanes] = split(values)


def build_tables(slabs, depths, forth, back, y_forth, y_back):
    grid_x, grid_z = CX * slabs, CZ * depths
    size = grid_x * grid_z
    first, second = slice(0, size), slice(size, 2 * size)
    for refs, freq_axis in ((forth, 0), (back, 1)):
        freq = index_like((size, size), freq_axis)
        cell = index_like((size, size), 1 - freq_axis)
        device, local = cell // (CX * CZ), cell % (CX * CZ)
        at_x = device // depths * CX + local // CZ
        at_z = device % depths * CZ + local % CZ
        turns = ((freq // grid_z * at_x) % grid_x).astype(F32) / grid_x
        turns = turns + ((freq % grid_z * at_z) % grid_z).astype(F32) / grid_z
        cosine, sine = cos_sin_wide(turns, 1.0)
        keep_halves(refs, first, first, cosine)
        keep_halves(refs, second, second, cosine)
        keep_halves(refs, first, second, -sine if freq_axis == 0 else sine)
        keep_halves(refs, second, first, sine if freq_axis == 0 else -sine)
    line = (NY, NY)
    turns = ((index_like(line, 0) * index_like(line, 1)) % NY).astype(F32) / NY
    cosine, sine = cos_sin_wide(turns, 1.0)
    first, second = slice(0, NY), slice(NY, 2 * NY)
    keep_halves(y_forth, first, first, cosine)
    keep_halves(y_forth, first, second, sine)
    keep_halves(y_back, first, first, cosine)
    keep_halves(y_back, second, first, sine)


def times_table(table, values):
    high, low = split(values)
    lanes = values.shape[1]
    both = dot(table[0], jnp.concatenate([high, low], 1))
    return both[:, :lanes] + both[:, lanes:] + dot(table[1], high)


def table_times(values, table):
    high, low = split(values)
    return dot(high, table[0]) + dot(low, table[0]) + dot(high, table[1])


def loaded(refs, rows=slice(None)):
    return tuple(ref[rows] for ref in refs)


def stage_forward(grid, forth, y_forth):
    lines = dot(grid.astype(BF), y_forth[0][...])
    size = grid.shape[0]
    wide = jnp.concatenate([lines[:, :NY], lines[:, NY:]], 0).astype(BF)
    out = dot(forth[0][...], wide)
    return out[:size], out[size:]


def stage_inverse(real_part, imag_part, table, y_back):
    out = times_table(table, jnp.concatenate([real_part, imag_part], 0))
    size = out.shape[0] // 2
    return table_times(jnp.concatenate([out[:size], out[size:]], 1), loaded(y_back))


def full_sum(values):
    return jnp.sum(jnp.sum(values, axis=0, keepdims=True), axis=1, keepdims=True)


def transfer_of(psf, grid_z, forth, y_forth):
    spec_re, spec_im = stage_forward(psf, forth, y_forth)
    row, lane = index_like(psf.shape, 0), index_like(psf.shape, 1)
    odd = (row // grid_z + row % grid_z + lane) % 2
    scale = (1.0 - 2.0 * odd.astype(F32)) / full_sum(psf)
    return spec_re * scale, spec_im * scale


def deconvolve(transfer, beam_hat, forth, back, y_forth, y_back, whole, own_rows):
    trans_re, trans_im = transfer
    beam_re, beam_im = beam_hat
    size = beam_re.shape[0]
    total = float(size * NY)
    power = trans_re * trans_re + trans_im * trans_im
    data_re = trans_re * beam_re + trans_im * beam_im
    data_im = trans_re * beam_im - trans_im * beam_re
    source = None
    for sweep in range(ITERS):
        if sweep == 0:
            grad_re, grad_im = -data_re, -data_im
        else:
            hat_re, hat_im = stage_forward(source, forth, y_forth)
            grad_re = power * hat_re - data_re
            grad_im = power * hat_im - data_im
        norm = grad_re * grad_re + grad_im * grad_im
        grad_norm = full_sum(norm) / total
        image_norm = full_sum(power * norm) / total
        step = grad_norm / (image_norm + 1e-06) / total
        if sweep < ITERS - 1:
            table = loaded(back)
        else:
            start, count = own_rows
            parts = [loaded(back, pl.ds(start + at, count)) for at in (0, size)]
            table = [jnp.concatenate([parts[0][half], parts[1][half]], 0) for half in range(2)]
            whole[...] = source
            source = whole[pl.ds(start, count)]
        move = step * stage_inverse(grad_re, grad_im, table, y_back)
        source = jnp.maximum(-move if sweep == 0 else source - move, 0.0)
    return source


def prepare(order, positions, centre, rates, near_x, near_z, near_y, bins, factor, mids):
    mics = order.shape[1]
    hot = (lax.broadcasted_iota(jnp.int32, (mics, mics), 0) == order[...]).astype(F32).astype(BF)
    values = jnp.concatenate([positions[...], jnp.zeros((5, mics), F32)], 0)
    high = values.astype(BF)
    mid_full = values - high.astype(F32)
    middle = mid_full.astype(BF)
    low = (mid_full - middle.astype(F32)).astype(BF)
    placed = dot(high, hot) + dot(middle, hot) + dot(low, hot)
    columns = placed.T
    wide = (mics, NY)
    near_x[...] = jnp.broadcast_to(columns[:, 0:1], wide)
    near_z[...] = jnp.broadcast_to(columns[:, 2:3], wide)
    y_value = coords_plane(lax.broadcasted_iota(jnp.int32, wide, 1), NY)
    diff = y_value - jnp.broadcast_to(columns[:, 1:2], wide)
    near_y[...] = diff * diff
    diff_x = centre[0] - placed[0:1]
    diff_y = centre[1] - placed[1:2]
    diff_z = centre[2] - placed[2:3]
    square = diff_x * diff_x + diff_y * diff_y + diff_z * diff_z
    dist = square * lax.rsqrt(square)
    for which in range(bins):
        cosine, sine = cos_sin(dist * rates[which], factor)
        rows = jnp.concatenate([cosine.astype(F32), sine.astype(F32), jnp.zeros((6, mics), F32)], 0)
        column = rows.T
        for part in range(2):
            mids[which, part] = jnp.broadcast_to(column[:, part : part + 1], wide)


def steer_rows(chunk, block, depth_start, slab, grid_x, grid_z, rates, near, store, bins, factor, mids, dots):
    near_x, near_z, near_y = near
    mics = near_x.shape[0]
    size = 64
    rows = pl.ds(pl.multiple_of(block * size, size), size)
    below = pl.ds(pl.multiple_of(mics + block * size, size), size)
    x_value = (2.0 * (slab * CX + chunk // (CZ // 2)).astype(F32) + 1.0) / grid_x - 1.0
    diff_x = x_value - near_x[rows]
    plane = diff_x * diff_x + near_y[rows]
    for half in range(2):
        depth = depth_start + chunk % (CZ // 2) * 2 + half
        z_value = 2.0 + (depth.astype(F32) + 0.5) / grid_z
        diff_z = z_value - near_z[rows]
        square = plane + diff_z * diff_z
        dist = square * lax.rsqrt(square)
        for which in range(bins):
            cosine, sine = cos_sin(dist * rates[which], factor)
            store[chunk, which, rows, half * NY : (half + 1) * NY] = cosine
            store[chunk, which, below, half * NY : (half + 1) * NY] = sine
            cosine, sine = cosine.astype(F32), sine.astype(F32)
            mid_re, mid_im = mids[which, 0, rows], mids[which, 1, rows]
            real_dot = cosine * mid_re + sine * mid_im
            imag_dot = cosine * mid_im - sine * mid_re
            for part, value in enumerate((real_dot, imag_dot)):
                folded = jnp.sum(value.reshape(size // 8, 8, NY), axis=0)
                dots[chunk, which, part, :, half * NY : (half + 1) * NY] += folded


def beam_chunk(chunk, which, spectra, store):
    mics = spectra.shape[2]
    steer_re = store[chunk, which, :mics]
    steer_im = store[chunk, which, mics:]
    first = dot(spectra[2 * which], steer_re) + dot(spectra[2 * which + 1], steer_im)
    second = dot(spectra[2 * which], steer_im)
    both = steer_re.astype(F32) * first + steer_im.astype(F32) * second
    return jnp.sum(both, axis=0, keepdims=True)


def spread_chunk(chunk, dots, bins):
    spread = jnp.zeros((1, 2 * NY), F32)
    for which in range(bins):
        for part in range(2):
            value = jnp.sum(dots[chunk, which, part], axis=0, keepdims=True)
            spread = spread + value * value / bins
    return spread


def put_chunk(ref, chunk, values):
    ref[chunk // 2, pl.ds(chunk % 2 * 2, 1)] = values[:, :NY]
    ref[chunk // 2, pl.ds(chunk % 2 * 2 + 1, 1)] = values[:, NY:]


RIGHT, LEFT, ACROSS, SIBLING = range(4)
MESH = pl.DeviceIdType.MESH


def centre_of(grid_x, grid_z):
    return (
        (2.0 * (grid_x // 2) + 1.0) / grid_x - 1.0,
        (2.0 * (NY // 2) + 1.0) / NY - 1.0,
        2.0 + (grid_z // 2 + 0.5) / grid_z,
    )


def whole_kernel(
    sizes,
    csm_in,
    positions_in,
    order_in,
    rates_in,
    beam_ref,
    source_ref,
    csm,
    positions,
    order,
    rates_ref,
    spectra,
    store,
    near_x,
    near_z,
    near_y,
    mids,
    dots,
    maps,
    own_psf,
    parts,
    forth_high,
    forth_low,
    back_high,
    back_low,
    y_forth_high,
    y_forth_low,
    y_back_high,
    y_back_low,
    whole,
    load_sem,
    block_sent,
    block_got,
    map_sent,
    map_got,
):
    forth, back = (forth_high, forth_low), (back_high, back_low)
    y_forth, y_back = (y_forth_high, y_forth_low), (y_back_high, y_back_low)
    size_x, size_y, size_z, bins = sizes
    grid_x, grid_z = CX * size_x, CZ * size_y * size_z
    mics = order.shape[1]
    share = csm.shape[2]
    devices = size_x * size_y * size_z
    factor = 1.0 / math.sqrt(mics)
    at_x, at_y, at_z = lax.axis_index("gx"), lax.axis_index("gy"), lax.axis_index("gz")

    def number(x, y, z):
        return (x * size_y + y) * size_z + z

    own = number(at_x, at_y, at_z)
    depth_start = (at_y * size_z + at_z) * CZ

    def place(device):
        return {
            "gx": device // (size_y * size_z),
            "gy": device // size_z % size_y,
            "gz": device % size_z,
        }

    barrier = pltpu.get_barrier_semaphore()

    def greet(i, carry):
        pl.semaphore_signal(
            barrier, inc=1, device_id=place((own + i) % devices), device_id_type=MESH
        )
        return carry

    lax.fori_loop(1, devices, greet, 0)
    loads = [
        pltpu.make_async_copy(source, target, load_sem.at[i])
        for i, (source, target) in enumerate(
            [(csm_in, csm), (positions_in, positions), (order_in, order), (rates_in, rates_ref)]
        )
    ]
    for load in loads:
        load.start()

    def rows_of(block):
        return pl.ds(pl.multiple_of(block * share, share), share)

    pieces = 2 * bins
    for load in loads:
        load.wait()
    for which in range(bins):
        spectra[2 * which, rows_of(own)] = csm[0, which]
        spectra[2 * which + 1, rows_of(own)] = (csm[1, which].astype(F32) * -2.0).astype(BF)
    pl.semaphore_wait(barrier, devices - 1)

    sends = []

    def block_copy(piece, block, way, target):
        view = spectra.at[piece, rows_of(block)]
        return pltpu.make_async_remote_copy(
            src_ref=view,
            dst_ref=view,
            send_sem=block_sent.at[way, piece, block],
            recv_sem=block_got.at[piece, block],
            device_id=target,
            device_id_type=MESH,
        )

    sibling, across = {"gz": 1 - at_z}, {"gy": 1 - at_y}

    def along(sign):
        return {"gx": at_x + sign}

    def send(valid, piece, block, way, target):
        sends.append((valid, piece, block, way, target))

        @pl.when(valid)
        def _():
            block_copy(piece, block, way, target).start()

    def await_block(valid, piece, block):
        @pl.when(valid)
        def _():
            block_copy(piece, block, SIBLING, sibling).wait_recv()

    def inside(x):
        return (x >= 0) & (x < size_x)

    always = at_x >= 0

    def from_line(piece, distance):
        for sign, way in ((1, RIGHT), (-1, LEFT)):
            source = at_x - sign * distance
            block = number(source, at_y, at_z)
            valid = inside(source)
            await_block(valid, piece, block)
            if distance < size_x - 1:
                send(valid & inside(at_x + sign), piece, block, way, along(sign))
            send(valid, piece, block, ACROSS, across)
            send(valid, piece, block, SIBLING, sibling)

    def from_across(piece, distance):
        for sign in (1, -1) if distance else (1,):
            source = at_x - sign * distance
            block = number(source, 1 - at_y, at_z)
            valid = inside(source)
            await_block(valid, piece, block)
            send(valid, piece, block, SIBLING, sibling)

    def send_own(piece):
        for sign, way in ((1, RIGHT), (-1, LEFT)):
            send(inside(at_x + sign), piece, own, way, along(sign))
        send(always, piece, own, ACROSS, across)
        send(always, piece, own, SIBLING, sibling)

    events = []
    for piece in range(pieces):
        late = 5.2 * (piece // 2) + 0.65 * (piece % 2)
        if piece >= 2:
            events.append((late - 2.6, piece // 2, send_own, piece))
        for distance in range(size_x):
            if distance:
                events.append((1.65 * distance + late, piece // 2, from_line, piece, distance))
            events.append((1.65 * (distance + 1) + late, piece // 2, from_across, piece, distance))
    events.sort(key=lambda event: event[0])
    first = 1 + max(i for i, event in enumerate(events) if event[1] == 0)
    events, later = events[:first], events[first:]

    def run(some):
        for event in some:
            event[2](*event[3:])

    for piece in range(2):
        send_own(piece)
    dots[...] = jnp.zeros_like(dots)
    rates = [rates_ref[0:1, which : which + 1] * (0.5 / math.pi) for which in range(bins)]
    prepare(
        order, positions, centre_of(grid_x, grid_z), rates, near_x, near_z, near_y, bins, factor, mids
    )
    near = (near_x, near_z, near_y)
    blocks = mics // 64
    chunks = CX * CZ // 2
    count = chunks * blocks
    step = 4

    def steer(i, carry):
        steer_rows(
            i // blocks, i % blocks, depth_start, at_x, grid_x, grid_z, rates, near, store, bins, factor, mids, dots
        )
        return carry

    done = 0
    for start in range(0, count, step):
        lax.fori_loop(start, start + step, steer, 0)
        upto = len(events) * (start + step) // (count + 3 * step)
        run(events[done:upto])
        done = upto
    for chunk in range(chunks):
        put_chunk(own_psf, chunk, spread_chunk(chunk, dots, bins))

    rows = CX * CZ

    def map_copy(kind, i, source):
        return pltpu.make_async_remote_copy(
            src_ref=maps.at[kind, source],
            dst_ref=maps.at[kind, source],
            send_sem=map_sent.at[kind, i],
            recv_sem=map_got.at[kind, source],
            device_id=place((own + i) % devices),
            device_id_type=MESH,
        )

    def spread_map(kind, values):
        maps[kind, own] = jnp.concatenate([values[x] for x in range(CX)], 0).astype(BF)

        def one(i, carry):
            map_copy(kind, i, own).start()
            return carry

        lax.fori_loop(1, devices, one, 0)

    def await_map(kind):
        def one(i, carry):
            map_copy(kind, i, (own + i) % devices).wait_recv()
            return carry

        lax.fori_loop(1, devices, one, 0)
        return maps[kind].reshape(devices * rows, NY)

    spread_map(0, own_psf[...])
    build_tables(size_x, size_y * size_z, forth, back, y_forth, y_back)
    run(events[done:])
    for which in range(bins):
        for piece in (2 * which, 2 * which + 1):
            for x in range(size_x):
                for y in range(size_y):
                    await_block(always, piece, number(x, y, 1 - at_z))

        def beam_step(chunk, carry):
            put_chunk(parts.at[which], chunk, beam_chunk(chunk, which, spectra, store))
            return carry

        if which == 0:
            for chunk in range(0, chunks, 2):
                lax.fori_loop(chunk, chunk + 2, beam_step, 0)
                run(later[len(later) * chunk // chunks : len(later) * (chunk + 2) // chunks])
        else:
            lax.fori_loop(0, chunks, beam_step, 0)
    total = parts[0]
    for which in range(1, bins):
        total = total + parts[which]
    beam_ref[...] = total
    spread_map(1, total)
    transfer = transfer_of(await_map(0).astype(F32), grid_z, forth, y_forth)
    beam_hat = stage_forward(await_map(1), forth, y_forth)
    own_rows = (pl.multiple_of(own * rows, rows), rows)
    source = deconvolve(transfer, beam_hat, forth, back, y_forth, y_back, whole, own_rows)
    for x in range(CX):
        source_ref[x] = source[x * CZ : (x + 1) * CZ]

    for valid, piece, block, way, target in sends:

        @pl.when(valid)
        def _():
            block_copy(piece, block, way, target).wait_send()

    def sent(i, carry):
        for kind in range(2):
            map_copy(kind, i, own).wait_send()
        return carry

    lax.fori_loop(1, devices, sent, 0)


def small_device(csm, positions, mic_order, wavenumbers):
    sizes = (lax.axis_size("gx"), lax.axis_size("gy"), lax.axis_size("gz"), csm.shape[1])
    bins, mics = csm.shape[1], csm.shape[3]
    rows = CX * CZ
    devices = sizes[0] * sizes[1] * sizes[2]
    size = devices * rows
    vmem = pl.BlockSpec(memory_space=pltpu.VMEM)
    beam, source = pl.pallas_call(
        functools.partial(whole_kernel, sizes),
        out_shape=[jax.ShapeDtypeStruct((CX, CZ, NY), F32)] * 2,
        in_specs=[pl.BlockSpec(memory_space=pltpu.HBM)] * 4,
        out_specs=[vmem, vmem],
        scratch_shapes=[
            pltpu.VMEM(csm.shape, BF),
            pltpu.VMEM(positions.shape, F32),
            pltpu.VMEM((1, mics), jnp.int32),
            pltpu.VMEM((1, bins), F32),
            pltpu.VMEM((2 * bins, mics, mics), BF),
            pltpu.VMEM((rows // 2, bins, 2 * mics, 2 * NY), BF),
            pltpu.VMEM((mics, NY), F32),
            pltpu.VMEM((mics, NY), F32),
            pltpu.VMEM((mics, NY), F32),
            pltpu.VMEM((bins, 2, mics, NY), F32),
            pltpu.VMEM((rows // 2, bins, 2, 8, 2 * NY), F32),
            pltpu.VMEM((2, devices, rows, NY), BF),
            pltpu.VMEM((CX, CZ, NY), F32),
            pltpu.VMEM((bins, CX, CZ, NY), F32),
            pltpu.VMEM((2 * size, 2 * size), BF),
            pltpu.VMEM((2 * size, 2 * size), BF),
            pltpu.VMEM((2 * size, 2 * size), BF),
            pltpu.VMEM((2 * size, 2 * size), BF),
            pltpu.VMEM((NY, 2 * NY), BF),
            pltpu.VMEM((NY, 2 * NY), BF),
            pltpu.VMEM((2 * NY, NY), BF),
            pltpu.VMEM((2 * NY, NY), BF),
            pltpu.VMEM((size, NY), F32),
            pltpu.SemaphoreType.DMA((4,)),
            pltpu.SemaphoreType.DMA((4, 2 * bins, devices)),
            pltpu.SemaphoreType.DMA((2 * bins, devices)),
            pltpu.SemaphoreType.DMA((2, devices)),
            pltpu.SemaphoreType.DMA((2, devices)),
        ],
        compiler_params=pltpu.CompilerParams(
            vmem_limit_bytes=60 * 1024 * 1024, collective_id=0, has_side_effects=True
        ),
        name="maps_and_sources",
    )(csm, positions, mic_order[None], wavenumbers[None])
    return beam, source


def solution(mesh):
    sizes = mesh.shape
    small = sizes["gx"] <= 4 and sizes["gy"] == 2 and sizes["gz"] == 2
    return jax.shard_map(
        small_device if small else on_device,
        mesh=mesh,
        in_specs=(P(None, "band", ("gx", "gy", "gz"), None), P(), P(), P("band")),
        out_specs=(P(("band", "gx"), ("gy", "gz"), None), P(("band", "gx"), ("gy", "gz"), None)),
        check_vma=False,
    )
```

```python
import functools
import math

import jax
import jax.numpy as jnp
import numpy as np
from jax import lax
from jax.experimental import pallas as pl
from jax.experimental.pallas import tpu as pltpu
from jax.sharding import PartitionSpec as P

NY = 128
CX = 4
CZ = 4
ITERS = 3


highest = lax.Precision.HIGHEST


def coords_plane(index, length):
    return (2.0 * index.astype(jnp.float32) + 1.0) / length - 1.0


def coords_depth(index, length):
    return 2.0 + (index.astype(jnp.float32) + 0.5) / length


def steering(cells, placed, rate, factor):
    diff_x = cells[0][None, :] - placed[0][:, None]
    diff_y = cells[1][None, :] - placed[1][:, None]
    diff_z = cells[2][None, :] - placed[2][:, None]
    dist = jnp.sqrt(diff_x * diff_x + diff_y * diff_y + diff_z * diff_z)
    phase = rate * dist
    return (
        (jnp.cos(phase) * factor).astype(jnp.bfloat16),
        (-jnp.sin(phase) * factor).astype(jnp.bfloat16),
    )


def tables(length):
    counter = jnp.arange(length, dtype=jnp.int32)
    angles = (
        2.0 * math.pi / length * (counter[:, None] * counter[None, :] % length).astype(jnp.float32)
    )
    return (jnp.cos(angles), jnp.sin(angles))


def along_axis(table, values, axis):
    formula = {1: "kj,sjbc->skbc", 2: "kj,sajc->sakc", 3: "kj,sabj->sabk"}
    return jnp.einsum(formula[axis], table, values, precision=highest)


def alternate(real_part, imag_part):
    paired = jnp.stack([real_part, imag_part], 1)
    return paired.reshape((2 * real_part.shape[0],) + real_part.shape[1:])


def transform(stack, axis, sign):
    cosine, sine = tables(stack.shape[axis])
    real_part = stack[0::2]
    imag_part = stack[1::2]
    new_real = along_axis(cosine, real_part, axis) - sign * along_axis(sine, imag_part, axis)
    new_imag = along_axis(cosine, imag_part, axis) + sign * along_axis(sine, real_part, axis)
    return alternate(new_real, new_imag)


def forward(signals):
    cosine, sine = tables(signals.shape[3])
    flat = signals.reshape(-1, signals.shape[3])
    real_part = jnp.dot(flat, cosine, precision=highest).reshape(signals.shape)
    imag_part = -jnp.dot(flat, sine, precision=highest).reshape(signals.shape)
    stack = alternate(real_part, imag_part)
    stack = lax.all_to_all(stack, "gx", split_axis=3, concat_axis=1, tiled=True)
    stack = transform(stack, 1, -1.0)
    stack = lax.all_to_all(stack, ("gy", "gz"), split_axis=1, concat_axis=2, tiled=True)
    stack = transform(stack, 2, -1.0)
    return stack


def inverse(stack, total):
    stack = transform(stack, 2, 1.0)
    stack = lax.all_to_all(stack, ("gy", "gz"), split_axis=2, concat_axis=1, tiled=True)
    stack = transform(stack, 1, 1.0)
    stack = lax.all_to_all(stack, "gx", split_axis=1, concat_axis=3, tiled=True)
    cosine, sine = tables(stack.shape[3])
    values = along_axis(cosine, stack[0::2], 3) - along_axis(sine, stack[1::2], 3)
    return values / total


def parity(first, second, third):
    summed = (first[:, None, None] + second[None, :, None] + third[None, None, :]) % 2
    return 1.0 - 2.0 * summed.astype(jnp.float32)


def on_device(csm, positions, mic_order, wavenumbers):
    size_x = lax.axis_size("gx")
    size_y = lax.axis_size("gy")
    size_z = lax.axis_size("gz")
    slab_index = lax.axis_index("gx")
    outer_index = lax.axis_index("gy")
    core_index = lax.axis_index("gz")
    depth_index = outer_index * size_z + core_index
    mics = csm.shape[3]
    bins = csm.shape[1]
    grid_x = CX * size_x
    grid_z = CZ * size_y * size_z
    factor = 1.0 / math.sqrt(mics)
    placed = jnp.take(positions, mic_order, axis=1)
    centre = jnp.stack(
        [
            coords_plane(jnp.full((1,), grid_x // 2, jnp.int32), grid_x),
            coords_plane(jnp.full((1,), NY // 2, jnp.int32), NY),
            coords_depth(jnp.full((1,), grid_z // 2, jnp.int32), grid_z),
        ]
    )
    centre_rows = []
    for which in range(bins):
        centre_re, centre_im = steering(centre, placed, wavenumbers[which], factor)
        centre_rows.append(jnp.concatenate([centre_re, centre_im], 1).T)
    spectra = lax.all_gather(csm, ("gx", "gy", "gz"), axis=2, tiled=True)
    depth_count = CZ
    depth_start = depth_index * CZ
    y_coords = coords_plane(jnp.arange(NY, dtype=jnp.int32), NY)
    z_coords = coords_depth(depth_start + jnp.arange(depth_count, dtype=jnp.int32), grid_z)
    count = depth_count * NY

    def plane(local):
        x_value = coords_plane(slab_index * CX + local, grid_x)
        cells = jnp.stack(
            [
                jnp.broadcast_to(x_value, (count,)),
                jnp.tile(y_coords, depth_count),
                jnp.repeat(z_coords, NY),
            ]
        )
        beam = jnp.zeros((count,), jnp.float32)
        spread = jnp.zeros((count,), jnp.float32)
        for which in range(bins):
            steer_re, steer_im = steering(cells, placed, wavenumbers[which], factor)
            both = jnp.concatenate([steer_re, steer_im], 1)
            first = jnp.dot(spectra[0, which], both, preferred_element_type=jnp.float32)
            second = jnp.dot(spectra[1, which], steer_im, preferred_element_type=jnp.float32)
            rows_re, rows_im = (steer_re, steer_im)
            rows_re = rows_re.astype(jnp.float32)
            rows_im = rows_im.astype(jnp.float32)
            beam = beam + jnp.sum(
                rows_re * first[:, :count] + rows_im * first[:, count:] - 2.0 * rows_re * second,
                axis=0,
            )
            dots = jnp.dot(centre_rows[which], both, preferred_element_type=jnp.float32)
            real_dot = dots[0, :count] + dots[1, count:]
            imag_dot = dots[1, :count] - dots[0, count:]
            spread = spread + (real_dot * real_dot + imag_dot * imag_dot) / bins
        return (beam, spread)

    beams, spreads = lax.map(plane, jnp.arange(CX, dtype=jnp.int32))
    beam_map = beams.reshape(CX, depth_count, NY)
    psf = spreads.reshape(CX, depth_count, NY)
    psf_sum = lax.psum(jnp.sum(psf), ("gx", "gy", "gz"))
    spectrum = forward(jnp.stack([psf, beam_map]))
    x_share = grid_x // (size_y * size_z)
    y_share = NY // size_x
    signs = parity(
        depth_index * x_share + jnp.arange(x_share, dtype=jnp.int32),
        jnp.arange(grid_z, dtype=jnp.int32),
        slab_index * y_share + jnp.arange(y_share, dtype=jnp.int32),
    )
    psf_real = spectrum[0] * signs / psf_sum
    psf_imag = spectrum[1] * signs / psf_sum
    beam_real = spectrum[2]
    beam_imag = spectrum[3]
    total = float(grid_x * NY * grid_z)
    source = jnp.zeros((CX, CZ, NY), jnp.float32)
    for sweep in range(ITERS):
        if sweep == 0:
            resid_real = -beam_real
            resid_imag = -beam_imag
        else:
            source_hat = forward(source[None])
            resid_real = psf_real * source_hat[0] - psf_imag * source_hat[1] - beam_real
            resid_imag = psf_real * source_hat[1] + psf_imag * source_hat[0] - beam_imag
        grad_real = psf_real * resid_real + psf_imag * resid_imag
        grad_imag = psf_real * resid_imag - psf_imag * resid_real
        image_real = psf_real * grad_real - psf_imag * grad_imag
        image_imag = psf_real * grad_imag + psf_imag * grad_real
        spaces = inverse(jnp.stack([grad_real, grad_imag, image_real, image_imag]), total)
        grad = spaces[0]
        image = spaces[1]
        grad_norm, image_norm = lax.psum(
            (jnp.sum(grad * grad), jnp.sum(image * image)), ("gx", "gy", "gz")
        )
        length = grad_norm / (image_norm + 1e-06)
        source = jnp.maximum(source - length * grad, 0.0)
    return (beam_map, source)


BF = jnp.bfloat16
F32 = jnp.float32


def fit_coeffs():
    theta = (np.cos(np.pi * (np.arange(4000) + 0.5) / 4000) + 1.0) * 0.5 * 0.25
    turns = np.sqrt(theta)
    cos_fit = np.polynomial.chebyshev.Chebyshev.fit(theta, np.cos(np.pi * turns), 3)
    sin_fit = np.polynomial.chebyshev.Chebyshev.fit(theta, np.sin(np.pi * turns) / turns, 3)
    to_power = lambda fit: fit.convert(kind=np.polynomial.Polynomial).coef
    return to_power(cos_fit), to_power(sin_fit)


COS_COEF, SIN_COEF = fit_coeffs()


def horner(values, coefs):
    total = float(coefs[-1]) * values + float(coefs[-2])
    for coef in coefs[-3::-1]:
        total = total * values + float(coef)
    return total


def cos_sin_wide(turns, factor):
    magic = float(1.5 * 2.0**23)
    rest = turns - ((turns + magic) - magic)
    square = rest * rest
    root = math.sqrt(2.0 * factor)
    half_sine = horner(square, SIN_COEF * root) * rest
    return factor - half_sine * half_sine, horner(square, COS_COEF * -root) * half_sine


def cos_sin(turns, factor):
    cosine, sine = cos_sin_wide(turns, factor)
    return cosine.astype(BF), sine.astype(BF)


def split(values):
    high = values.astype(BF)
    return high, (values - high.astype(F32)).astype(BF)


def dot(first, second):
    return jnp.dot(first, second, preferred_element_type=F32)


def index_like(shape, axis):
    return lax.broadcasted_iota(jnp.int32, shape, axis)


def keep_halves(refs, rows, lanes, values):
    refs[0][rows, lanes], refs[1][rows, lanes] = split(values)


def build_tables(slabs, depths, forth, back, y_forth, y_back):
    grid_x, grid_z = CX * slabs, CZ * depths
    size = grid_x * grid_z
    first, second = slice(0, size), slice(size, 2 * size)
    for refs, freq_axis in ((forth, 0), (back, 1)):
        freq = index_like((size, size), freq_axis)
        cell = index_like((size, size), 1 - freq_axis)
        device, local = cell // (CX * CZ), cell % (CX * CZ)
        at_x = device // depths * CX + local // CZ
        at_z = device % depths * CZ + local % CZ
        turns = ((freq // grid_z * at_x) % grid_x).astype(F32) / grid_x
        turns = turns + ((freq % grid_z * at_z) % grid_z).astype(F32) / grid_z
        cosine, sine = cos_sin_wide(turns, 1.0)
        keep_halves(refs, first, first, cosine)
        keep_halves(refs, second, second, cosine)
        keep_halves(refs, first, second, -sine if freq_axis == 0 else sine)
        keep_halves(refs, second, first, sine if freq_axis == 0 else -sine)
    line = (NY, NY)
    turns = ((index_like(line, 0) * index_like(line, 1)) % NY).astype(F32) / NY
    cosine, sine = cos_sin_wide(turns, 1.0)
    first, second = slice(0, NY), slice(NY, 2 * NY)
    keep_halves(y_forth, first, first, cosine)
    keep_halves(y_forth, first, second, sine)
    keep_halves(y_back, first, first, cosine)
    keep_halves(y_back, second, first, sine)


def times_table(table, values):
    high, low = split(values)
    lanes = values.shape[1]
    both = dot(table[0], jnp.concatenate([high, low], 1))
    return both[:, :lanes] + both[:, lanes:] + dot(table[1], high)


def table_times(values, table):
    high, low = split(values)
    return dot(high, table[0]) + dot(low, table[0]) + dot(high, table[1])


def loaded(refs, rows=slice(None)):
    return tuple(ref[rows] for ref in refs)


def stage_forward(grid, forth, y_forth):
    lines = dot(grid.astype(BF), y_forth[0][...])
    size = grid.shape[0]
    wide = jnp.concatenate([lines[:, :NY], lines[:, NY:]], 0).astype(BF)
    out = dot(forth[0][...], wide)
    return out[:size], out[size:]


def stage_inverse(real_part, imag_part, table, y_back):
    out = times_table(table, jnp.concatenate([real_part, imag_part], 0))
    size = out.shape[0] // 2
    return table_times(jnp.concatenate([out[:size], out[size:]], 1), loaded(y_back))


def full_sum(values):
    return jnp.sum(jnp.sum(values, axis=0, keepdims=True), axis=1, keepdims=True)


def transfers_of(psf, beam, grid_z, forth, y_forth):
    size = psf.shape[0]
    lines = dot(jnp.concatenate([psf, beam], 0), y_forth[0][...])
    grids = [
        jnp.concatenate([part[:, :NY], part[:, NY:]], 0) for part in (lines[:size], lines[size:])
    ]
    out = dot(forth[0][...], jnp.concatenate(grids, 1).astype(BF))
    row, lane = index_like(psf.shape, 0), index_like(psf.shape, 1)
    odd = (row // grid_z + row % grid_z + lane) % 2
    scale = (1.0 - 2.0 * odd.astype(F32)) / full_sum(psf.astype(F32))
    transfer = (out[:size, :NY] * scale, out[size:, :NY] * scale)
    return transfer, (out[:size, NY:], out[size:, NY:])


def deconvolve(transfer, beam_hat, forth, back, y_forth, y_back, whole, own_rows):
    trans_re, trans_im = transfer
    beam_re, beam_im = beam_hat
    size = beam_re.shape[0]
    total = float(size * NY)
    power = trans_re * trans_re + trans_im * trans_im
    data_re = trans_re * beam_re + trans_im * beam_im
    data_im = trans_re * beam_im - trans_im * beam_re
    source = None
    for sweep in range(ITERS):
        if sweep == 0:
            grad_re, grad_im = -data_re, -data_im
        else:
            hat_re, hat_im = stage_forward(source, forth, y_forth)
            grad_re = power * hat_re - data_re
            grad_im = power * hat_im - data_im
        norm = grad_re * grad_re + grad_im * grad_im
        grad_norm = full_sum(norm) / total
        image_norm = full_sum(power * norm) / total
        step = grad_norm / (image_norm + 1e-06) / total
        if sweep < ITERS - 1:
            table = loaded(back)
        else:
            start, count = own_rows
            parts = [loaded(back, pl.ds(start + at, count)) for at in (0, size)]
            table = [jnp.concatenate([parts[0][half], parts[1][half]], 0) for half in range(2)]
            whole[...] = source
            source = whole[pl.ds(start, count)]
        move = step * stage_inverse(grad_re, grad_im, table, y_back)
        source = jnp.maximum(-move if sweep == 0 else source - move, 0.0)
    return source


def prepare(order, positions, centre, rates, near_x, near_z, near_y, bins, factor, spectra):
    mics = order.shape[1]
    hot = (lax.broadcasted_iota(jnp.int32, (mics, mics), 0) == order[...]).astype(F32).astype(BF)
    values = jnp.concatenate([positions[...], jnp.zeros((5, mics), F32)], 0)
    high = values.astype(BF)
    mid_full = values - high.astype(F32)
    middle = mid_full.astype(BF)
    low = (mid_full - middle.astype(F32)).astype(BF)
    placed = dot(high, hot) + dot(middle, hot) + dot(low, hot)
    columns = placed.T
    wide = (mics, NY)
    near_x[...] = jnp.broadcast_to(columns[:, 0:1], wide)
    near_z[...] = jnp.broadcast_to(columns[:, 2:3], wide)
    y_value = coords_plane(lax.broadcasted_iota(jnp.int32, wide, 1), NY)
    diff = y_value - jnp.broadcast_to(columns[:, 1:2], wide)
    near_y[...] = diff * diff
    diff_x = centre[0] - placed[0:1]
    diff_y = centre[1] - placed[1:2]
    diff_z = centre[2] - placed[2:3]
    square = diff_x * diff_x + diff_y * diff_y + diff_z * diff_z
    dist = square * lax.rsqrt(square)
    for which in range(bins):
        cosine, sine = cos_sin(dist * rates[which], factor)
        rows = [cosine.astype(F32), sine.astype(F32), jnp.zeros((14, mics), F32)]
        spectra[2 * which, pl.ds(mics, 16)] = jnp.concatenate(rows, 0).astype(BF)


def steer_rows(chunk, block, depth_start, slab, grid_x, grid_z, rates, near, store, bins, factor):
    near_x, near_z, near_y = near
    mics = near_x.shape[0]
    size = 128
    rows = pl.ds(pl.multiple_of(block * size, size), size)
    below = pl.ds(pl.multiple_of(mics + block * size, size), size)
    x_value = (2.0 * (slab * CX + chunk // (CZ // 2)).astype(F32) + 1.0) / grid_x - 1.0
    diff_x = x_value - near_x[rows]
    plane = diff_x * diff_x + near_y[rows]
    for half in range(2):
        depth = depth_start + chunk % (CZ // 2) * 2 + half
        z_value = 2.0 + (depth.astype(F32) + 0.5) / grid_z
        diff_z = z_value - near_z[rows]
        square = plane + diff_z * diff_z
        dist = square * lax.rsqrt(square)
        for which in range(bins):
            cosine, sine = cos_sin(dist * rates[which], factor)
            store[chunk, which, rows, half * NY : (half + 1) * NY] = cosine
            store[chunk, which, below, half * NY : (half + 1) * NY] = sine


def map_chunk(chunk, which, spectra, store, bins):
    mics = spectra.shape[2]
    steer_re = store[chunk, which, :mics]
    steer_im = store[chunk, which, mics:]
    by_re = dot(spectra[2 * which], steer_re)
    by_im = dot(spectra[2 * which], steer_im)
    first = by_re[:mics] + dot(spectra[2 * which + 1, :mics], steer_im)
    both = steer_re.astype(F32) * first + steer_im.astype(F32) * by_im[:mics]
    real_dot = by_re[mics : mics + 1] + by_im[mics + 1 : mics + 2]
    imag_dot = by_re[mics + 1 : mics + 2] - by_im[mics : mics + 1]
    spread = (real_dot * real_dot + imag_dot * imag_dot) / bins
    return jnp.sum(both, axis=0, keepdims=True), spread


def put_chunk(ref, chunk, values):
    ref[chunk // 2, pl.ds(chunk % 2 * 2, 1)] = values[:, :NY]
    ref[chunk // 2, pl.ds(chunk % 2 * 2 + 1, 1)] = values[:, NY:]


RIGHT, LEFT, ACROSS, SIBLING = range(4)
MESH = pl.DeviceIdType.MESH


def centre_of(grid_x, grid_z):
    return (
        (2.0 * (grid_x // 2) + 1.0) / grid_x - 1.0,
        (2.0 * (NY // 2) + 1.0) / NY - 1.0,
        2.0 + (grid_z // 2 + 0.5) / grid_z,
    )


def whole_kernel(
    sizes,
    csm_in,
    positions_in,
    order_in,
    rates_in,
    beam_ref,
    source_ref,
    csm,
    positions,
    order,
    rates_ref,
    spectra,
    store,
    near_x,
    near_z,
    near_y,
    maps,
    parts,
    forth_high,
    forth_low,
    back_high,
    back_low,
    y_forth_high,
    y_forth_low,
    y_back_high,
    y_back_low,
    whole,
    load_sem,
    block_sent,
    block_got,
    map_sent,
    map_got,
):
    forth, back = (forth_high, forth_low), (back_high, back_low)
    y_forth, y_back = (y_forth_high, y_forth_low), (y_back_high, y_back_low)
    size_x, size_y, size_z, bins = sizes
    grid_x, grid_z = CX * size_x, CZ * size_y * size_z
    mics = order.shape[1]
    share = csm.shape[2]
    devices = size_x * size_y * size_z
    factor = 1.0 / math.sqrt(mics)
    at_x, at_y, at_z = lax.axis_index("gx"), lax.axis_index("gy"), lax.axis_index("gz")

    def number(x, y, z):
        return (x * size_y + y) * size_z + z

    own = number(at_x, at_y, at_z)
    depth_start = (at_y * size_z + at_z) * CZ

    def place(device):
        return {
            "gx": device // (size_y * size_z),
            "gy": device // size_z % size_y,
            "gz": device % size_z,
        }

    barrier = pltpu.get_barrier_semaphore()

    def greet(i, carry):
        pl.semaphore_signal(
            barrier, inc=1, device_id=place((own + i) % devices), device_id_type=MESH
        )
        return carry

    lax.fori_loop(1, devices, greet, 0)
    loads = [
        pltpu.make_async_copy(source, target, load_sem.at[i])
        for i, (source, target) in enumerate(
            [(csm_in, csm), (positions_in, positions), (order_in, order), (rates_in, rates_ref)]
        )
    ]
    for load in loads:
        load.start()

    def rows_of(block):
        return pl.ds(pl.multiple_of(block * share, share), share)

    pieces = 2 * bins
    for load in loads:
        load.wait()
    for which in range(bins):
        spectra[2 * which, rows_of(own)] = csm[0, which]
        spectra[2 * which + 1, rows_of(own)] = (csm[1, which].astype(F32) * -2.0).astype(BF)
    pl.semaphore_wait(barrier, devices - 1)

    sends = []

    def block_copy(piece, block, way, target):
        view = spectra.at[piece, rows_of(block)]
        return pltpu.make_async_remote_copy(
            src_ref=view,
            dst_ref=view,
            send_sem=block_sent.at[way, piece, block],
            recv_sem=block_got.at[piece, block],
            device_id=target,
            device_id_type=MESH,
        )

    sibling, across = {"gz": 1 - at_z}, {"gy": 1 - at_y}

    def along(sign):
        return {"gx": at_x + sign}

    def send(valid, piece, block, way, target):
        sends.append((valid, piece, block, way, target))

        @pl.when(valid)
        def _():
            block_copy(piece, block, way, target).start()

    def await_block(valid, piece, block):
        @pl.when(valid)
        def _():
            block_copy(piece, block, SIBLING, sibling).wait_recv()

    def inside(x):
        return (x >= 0) & (x < size_x)

    always = at_x >= 0

    def from_line(piece, distance):
        for sign, way in ((1, RIGHT), (-1, LEFT)):
            source = at_x - sign * distance
            block = number(source, at_y, at_z)
            valid = inside(source)
            await_block(valid, piece, block)
            if distance < size_x - 1:
                send(valid & inside(at_x + sign), piece, block, way, along(sign))
            send(valid, piece, block, ACROSS, across)
            send(valid, piece, block, SIBLING, sibling)

    def from_across(piece, distance):
        for sign in (1, -1) if distance else (1,):
            source = at_x - sign * distance
            block = number(source, 1 - at_y, at_z)
            valid = inside(source)
            await_block(valid, piece, block)
            send(valid, piece, block, SIBLING, sibling)

    events = []
    for piece in range(pieces):
        for distance in range(size_x):
            if distance:
                events.append((1.65 * distance + 0.65 * piece, from_line, piece, distance))
            events.append((1.65 + 2.6 * distance + 0.65 * piece, from_across, piece, distance))
    events.sort(key=lambda event: event[0])

    for piece in range(pieces):
        for sign, way in ((1, RIGHT), (-1, LEFT)):
            send(inside(at_x + sign), piece, own, way, along(sign))
        send(always, piece, own, ACROSS, across)
        send(always, piece, own, SIBLING, sibling)
    rates = [rates_ref[0:1, which : which + 1] * (0.5 / math.pi) for which in range(bins)]
    prepare(
        order, positions, centre_of(grid_x, grid_z), rates, near_x, near_z, near_y, bins, factor, spectra
    )
    near = (near_x, near_z, near_y)
    blocks = mics // 128
    chunks = CX * CZ // 2
    count = chunks * blocks
    step = 2

    def steer(i, carry):
        steer_rows(
            i // blocks, i % blocks, depth_start, at_x, grid_x, grid_z, rates, near, store, bins, factor
        )
        return carry

    done = 0
    for start in range(0, count, step):
        lax.fori_loop(start, start + step, steer, 0)
        while done < len(events) * (start + step) // (count + 3 * step):
            events[done][1](*events[done][2:])
            done += 1
    build_tables(size_x, size_y * size_z, forth, back, y_forth, y_back)
    for event in events[done:]:
        event[1](*event[2:])

    rows = CX * CZ

    for which in range(bins):
        for piece in (2 * which, 2 * which + 1):
            for x in range(size_x):
                for y in range(size_y):
                    await_block(always, piece, number(x, y, 1 - at_z))

        def map_step(chunk, carry):
            beam, spread = map_chunk(chunk, which, spectra, store, bins)
            put_chunk(parts.at[which, 0], chunk, beam)
            put_chunk(parts.at[which, 1], chunk, spread)
            return carry

        lax.fori_loop(0, chunks, map_step, 0)
    for kind in range(2):
        total = parts[0, kind]
        for which in range(1, bins):
            total = total + parts[which, kind]
        maps[own, kind] = jnp.concatenate([total[x] for x in range(CX)], 0).astype(BF)
        if kind == 0:
            beam_ref[...] = total

    def map_copy(i, source):
        return pltpu.make_async_remote_copy(
            src_ref=maps.at[source],
            dst_ref=maps.at[source],
            send_sem=map_sent.at[i],
            recv_sem=map_got.at[source],
            device_id=place((own + i) % devices),
            device_id_type=MESH,
        )

    def spread_map(i, carry):
        map_copy(i, own).start()
        return carry

    def await_map(i, carry):
        map_copy(i, (own + i) % devices).wait_recv()
        return carry

    lax.fori_loop(1, devices, spread_map, 0)
    lax.fori_loop(1, devices, await_map, 0)
    size = devices * rows
    beam = maps[:, 0].reshape(size, NY)
    psf = maps[:, 1].reshape(size, NY)
    transfer, beam_hat = transfers_of(psf, beam, grid_z, forth, y_forth)
    own_rows = (pl.multiple_of(own * rows, rows), rows)
    source = deconvolve(transfer, beam_hat, forth, back, y_forth, y_back, whole, own_rows)
    for x in range(CX):
        source_ref[x] = source[x * CZ : (x + 1) * CZ]

    for valid, piece, block, way, target in sends:

        @pl.when(valid)
        def _():
            block_copy(piece, block, way, target).wait_send()

    def sent(i, carry):
        map_copy(i, own).wait_send()
        return carry

    lax.fori_loop(1, devices, sent, 0)


def small_device(csm, positions, mic_order, wavenumbers):
    sizes = (lax.axis_size("gx"), lax.axis_size("gy"), lax.axis_size("gz"), csm.shape[1])
    bins, mics = csm.shape[1], csm.shape[3]
    rows = CX * CZ
    devices = sizes[0] * sizes[1] * sizes[2]
    size = devices * rows
    vmem = pl.BlockSpec(memory_space=pltpu.VMEM)
    beam, source = pl.pallas_call(
        functools.partial(whole_kernel, sizes),
        out_shape=[jax.ShapeDtypeStruct((CX, CZ, NY), F32)] * 2,
        in_specs=[pl.BlockSpec(memory_space=pltpu.HBM)] * 4,
        out_specs=[vmem, vmem],
        scratch_shapes=[
            pltpu.VMEM(csm.shape, BF),
            pltpu.VMEM(positions.shape, F32),
            pltpu.VMEM((1, mics), jnp.int32),
            pltpu.VMEM((1, bins), F32),
            pltpu.VMEM((2 * bins, mics + 16, mics), BF),
            pltpu.VMEM((rows // 2, bins, 2 * mics, 2 * NY), BF),
            pltpu.VMEM((mics, NY), F32),
            pltpu.VMEM((mics, NY), F32),
            pltpu.VMEM((mics, NY), F32),
            pltpu.VMEM((devices, 2, rows, NY), BF),
            pltpu.VMEM((bins, 2, CX, CZ, NY), F32),
            pltpu.VMEM((2 * size, 2 * size), BF),
            pltpu.VMEM((2 * size, 2 * size), BF),
            pltpu.VMEM((2 * size, 2 * size), BF),
            pltpu.VMEM((2 * size, 2 * size), BF),
            pltpu.VMEM((NY, 2 * NY), BF),
            pltpu.VMEM((NY, 2 * NY), BF),
            pltpu.VMEM((2 * NY, NY), BF),
            pltpu.VMEM((2 * NY, NY), BF),
            pltpu.VMEM((size, NY), F32),
            pltpu.SemaphoreType.DMA((4,)),
            pltpu.SemaphoreType.DMA((4, 2 * bins, devices)),
            pltpu.SemaphoreType.DMA((2 * bins, devices)),
            pltpu.SemaphoreType.DMA((devices,)),
            pltpu.SemaphoreType.DMA((devices,)),
        ],
        compiler_params=pltpu.CompilerParams(
            vmem_limit_bytes=60 * 1024 * 1024, collective_id=0, has_side_effects=True
        ),
        name="maps_and_sources",
    )(csm, positions, mic_order[None], wavenumbers[None])
    return beam, source


def solution(mesh):
    sizes = mesh.shape
    small = sizes["gx"] <= 4 and sizes["gy"] == 2 and sizes["gz"] == 2
    return jax.shard_map(
        small_device if small else on_device,
        mesh=mesh,
        in_specs=(P(None, "band", ("gx", "gy", "gz"), None), P(), P(), P("band")),
        out_specs=(P(("band", "gx"), ("gy", "gz"), None), P(("band", "gx"), ("gy", "gz"), None)),
        check_vma=False,
    )
```
